512 devices in a mesh: win: 32 (over y, z_hi, x), tile: 16 (over z_lo, core).
Axes of the slice: x: 4, y: 4, z: 16 (z_hi: 2, z_lo: 8; z = z_hi * 8 + z_lo), core: 2. Of those that a mesh axis runs over, the one named last changes fastest.
Arguments:
- latents: bfloat16 [32, 16, 16, 2, 20, 320], P('win', None, 'tile'), may hold values from -40 to 40
- spatial_weight: bfloat16 [3, 3, 320, 320], replicated, may hold values from -0.109375 to 0.109375
- temporal_weight: bfloat16 [3, 320, 320], replicated, may hold values from -0.1875 to 0.1875
- gain_first: float32 [320], replicated, may hold values from 0.5 to 1.5
- shift_first: float32 [320], replicated, may hold values from -0.5 to 0.5
- gain_second: float32 [320], replicated, may hold values from 0.5 to 1.5
- shift_second: float32 [320], replicated, may hold values from -0.5 to 0.5
- temporal_bias: float32 [320], replicated, may hold values from -0.5 to 0.5
- starts: int32 [32], replicated, may hold values from 0 to 310, as said below
- blend_counts: int32 [32, 16], replicated, may hold values from 1 to 8
Outputs:
- joined: bfloat16 [32, 16, 16, 2, 20, 320], P('win', None, 'tile')
The draws below stay inside these ranges and needn't reach their ends.
Inputs may be any that keep to these rules, and one draw needn't show every extreme that they name: starts[0] is 0; consecutive starts rise by 8 to 12, by exactly 8 for at least one pair and by exactly 12 for at least one other pair; the last start is 310.
All inputs are finite; a program needn't handle non-finite values.
Results may differ from the reference program's by a relative error of at most 0.007.
Values may be sent and summed in bfloat16 or wider, within the bound.
A program may use at most 64 MiB of HBM per device.

```python
import jax
import jax.numpy as jnp
from jax import lax

C = 320
NORM_GROUPS = 32
FRAMES = 16
SHARED_FRAMES = 8
TCOLS = 4
TH = 2
TW = 20
TILES = 16
TROWS = 4
WINDOWS = 32


def draw_latents(key, part):
    key = jax.random.fold_in(key, 11)
    first = jax.random.fold_in(key, 0)
    second = jax.random.fold_in(key, 1)
    third = jax.random.fold_in(key, 2)
    fifth = jax.random.fold_in(key, 4)
    sixth = jax.random.fold_in(key, 5)
    shape = (WINDOWS, FRAMES, TILES, TH, TW, C)
    rising = 3.0 ** (jnp.arange(TILES).astype(jnp.float32) / max(TILES - 1, 1))
    window_keys = jax.random.split(fifth, WINDOWS)
    ordered = jax.vmap(lambda single: jax.random.permutation(single, rising))(window_keys)
    tile_scale = ordered.reshape(WINDOWS, 1, TILES, 1, 1, 1)
    tile_offset = jax.random.uniform(sixth, (WINDOWS, 1, TILES, 1, 1, 1), jnp.float32, -1.5, 1.5)
    channel_scale = jnp.exp(jax.random.uniform(second, (C,), jnp.float32, -0.7, 0.7))
    channel_mean = jax.random.uniform(third, (C,), jnp.float32, -1.0, 1.0)
    base = jnp.clip(jax.random.normal(first, shape, jnp.float32), -6.0, 6.0)
    drawn = base * tile_scale * channel_scale + channel_mean + tile_offset
    return drawn.astype(jnp.bfloat16)


def draw_starts(key, part):
    key = jax.random.fold_in(key, 23)
    first, second = jax.random.split(key, 2)
    gaps = WINDOWS - 1
    half = gaps // 2
    paired = jax.random.randint(first, (half,), SHARED_FRAMES, SHARED_FRAMES + 5)
    paired = paired.at[0].set(SHARED_FRAMES)
    middle = jnp.full((gaps - 2 * half,), SHARED_FRAMES + 2, jnp.int32)
    strides = jnp.concatenate([paired, 2 * SHARED_FRAMES + 4 - paired, middle]).astype(jnp.int32)
    order = jax.random.permutation(second, gaps)
    strides = strides[order]
    opening = jnp.zeros((1,), jnp.int32)
    return jnp.concatenate([opening, jnp.cumsum(strides).astype(jnp.int32)]).astype(jnp.int32)


def with_ends(entries, own_key, low, largest):
    extent = entries.shape
    index_at = [jax.random.randint(jax.random.fold_in(own_key, axis), (), 0, extent[axis]) for axis in range(len(extent))]
    entries = entries.at[tuple(index_at)].set(low)
    longest = extent.index(max(extent))
    index_at[longest] = (index_at[longest] + 1) % extent[longest]
    return entries.at[tuple(index_at)].set(largest)


def noise(own_key, extent, scale, limit, held_as=jnp.bfloat16):
    return jnp.clip(scale * jax.random.normal(own_key, extent, jnp.float32), -limit, limit).astype(held_as)


def setup_inputs(seed: int = 0) -> dict:
    keys = jax.random.split(jax.random.key(seed), 11)
    return {
        "latents": draw_latents(jax.random.fold_in(keys[10], 71), 0),
        "spatial_weight": noise(keys[1], (3, 3, C, C), (9 * C) ** -0.5, 0.109375),
        "temporal_weight": noise(keys[2], (3, C, C), (3 * C) ** -0.5, 0.1875),
        "gain_first": jnp.clip(jax.random.uniform(keys[3], (C,), jnp.float32, 0.5, 1.5), 0.5, 1.5),
        "shift_first": jnp.clip(jax.random.uniform(keys[4], (C,), jnp.float32, -0.5, 0.5), -0.5, 0.5),
        "gain_second": jnp.clip(jax.random.uniform(keys[5], (C,), jnp.float32, 0.5, 1.5), 0.5, 1.5),
        "shift_second": jnp.clip(jax.random.uniform(keys[6], (C,), jnp.float32, -0.5, 0.5), -0.5, 0.5),
        "temporal_bias": jnp.clip(jax.random.uniform(keys[7], (C,), jnp.float32, -0.5, 0.5), -0.5, 0.5),
        "starts": draw_starts(jax.random.fold_in(keys[10], 71), 0),
        "blend_counts": with_ends(jax.random.randint(keys[9], (WINDOWS, FRAMES), 1, 9), jax.random.fold_in(keys[9], 1), 1, 8).astype(jnp.int32),
    }


EPSILON = 1e-05

def grouped_normalise(field, gain, shift):
    channels = field.shape[-1]
    grouped = field.reshape(-1, NORM_GROUPS, channels // NORM_GROUPS)
    members = grouped.shape[0] * grouped.shape[2]
    group_mean = lax.optimization_barrier(jnp.sum(grouped, axis=(0, 2))) / members
    spread = lax.optimization_barrier(jnp.sum(grouped * grouped, axis=(0, 2))) / members - group_mean * group_mean
    inverse = lax.rsqrt(spread + EPSILON)
    return (field - jnp.repeat(group_mean, channels // NORM_GROUPS)) * jnp.repeat(inverse, channels // NORM_GROUPS) * gain + shift

def to_image(tiled):
    shaped = tiled.reshape(FRAMES, TROWS, TCOLS, TH, TW, C)
    return shaped.transpose(0, 1, 3, 2, 4, 5).reshape(FRAMES, TROWS * TH, TCOLS * TW, C)

def to_tiles(image):
    shaped = image.reshape(FRAMES, TROWS, TH, TCOLS, TW, C)
    return shaped.transpose(0, 1, 3, 2, 4, 5).reshape(FRAMES, TROWS * TCOLS, TH, TW, C)

def reference(latents, spatial_weight, temporal_weight, gain_first, shift_first, gain_second, shift_second, temporal_bias, starts, blend_counts):
    height = TROWS * TH
    across = TCOLS * TW

    def residual_block(latents_per_window):
        image = to_image(latents_per_window).astype(jnp.float32)
        activated = jax.nn.silu(grouped_normalise(image, gain_first, shift_first)).astype(jnp.bfloat16)
        padded = jnp.pad(activated, ((0, 0), (1, 1), (1, 1), (0, 0)))
        summed = jnp.zeros((FRAMES * height * across, C), jnp.float32)
        for offset_row in range(3):
            for offset_col in range(3):
                piece = padded[:, offset_row:offset_row + height, offset_col:offset_col + across].reshape(-1, C)
                summed = summed + jnp.dot(piece, spatial_weight[offset_row, offset_col], preferred_element_type=jnp.float32)
        spatial = summed.astype(jnp.bfloat16).reshape(FRAMES, height, across, C)
        mixed = jax.nn.silu(grouped_normalise(spatial.astype(jnp.float32), gain_second, shift_second)).astype(jnp.bfloat16)
        flat = mixed.reshape(FRAMES, height * across, C)
        empty = jnp.zeros((1, height * across, C), jnp.bfloat16)
        framed = jnp.concatenate([empty, flat, empty], axis=0)
        running = image.reshape(-1, C) + temporal_bias
        for tap in range(3):
            running = running + jnp.dot(framed[tap:tap + FRAMES].reshape(-1, C), temporal_weight[tap], preferred_element_type=jnp.float32)
        block = running.astype(jnp.bfloat16).reshape(FRAMES, height, across, C)
        return to_tiles(block)
    residual_blocks = lax.map(residual_block, latents)

    def join(index):
        own = residual_blocks[index].astype(jnp.float32)
        prev_index = jnp.maximum(index - 1, 0)
        next_index = jnp.minimum(index + 1, WINDOWS - 1)
        frame_ids = jnp.arange(FRAMES).astype(jnp.int32)
        prev_frame = frame_ids + starts[index] - starts[prev_index]
        prev_ok = (index > 0) & (prev_frame <= FRAMES - 1)
        prev_clip = jnp.clip(prev_frame, 0, FRAMES - 1).astype(jnp.int32)
        prev_weight = jnp.where(prev_ok, blend_counts[prev_index][prev_clip], 0).astype(jnp.float32)
        next_frame = frame_ids - (starts[next_index] - starts[index])
        next_ok = (index < WINDOWS - 1) & (next_frame >= 0)
        next_clip = jnp.clip(next_frame, 0, FRAMES - 1).astype(jnp.int32)
        next_weight = jnp.where(next_ok, blend_counts[next_index][next_clip], 0).astype(jnp.float32)
        own_weight = blend_counts[index].astype(jnp.float32)
        prev_frames = residual_blocks[prev_index][prev_clip].astype(jnp.float32)
        next_frames = residual_blocks[next_index][next_clip].astype(jnp.float32)
        expand = (slice(None), None, None, None, None)
        numer = own_weight[expand] * own + prev_weight[expand] * prev_frames + next_weight[expand] * next_frames
        denom = own_weight + prev_weight + next_weight
        return (numer / denom[expand]).astype(jnp.bfloat16)
    return lax.map(join, jnp.arange(WINDOWS).astype(jnp.int32))
```

```python
import jax
import jax.numpy as jnp
from jax import lax
from jax.experimental import pallas as pl
from jax.experimental.pallas import tpu as pltpu
from jax.sharding import PartitionSpec as P

MESH = pl.DeviceIdType.MESH
F32 = jnp.float32
BF16 = jnp.bfloat16

GROUPS = 32
EPSILON = 1e-05
FRAMES = 16
SHARED = 8
TCOLS = 4
TROWS = 4
TILES = TCOLS * TROWS
WINDOWS = 32
COLS = 20
C = 320
HALF = 256
PIX = COLS * FRAMES
WIDE = (COLS + 2) * FRAMES
MEMBERS = float(FRAMES * TILES * 2 * COLS * (C // GROUPS))


def pack_rest(field):
    half = field.shape[0] // 2
    return jnp.concatenate([field[:half, HALF:], field[half:, HALF:]], axis=1)


def unpack_rest(rest):
    return jnp.concatenate([rest[:, : C - HALF], rest[:, C - HALF :]], axis=0)


def exact_dot(rows, ones):
    high = rows.astype(BF16).astype(F32)
    rest = rows - high
    middle = rest.astype(BF16).astype(F32)
    low = rest - middle
    parts = jnp.concatenate([high, middle, low, jnp.zeros_like(low)], axis=0)
    product = jnp.dot(parts.astype(BF16), ones, preferred_element_type=F32)
    return product[0:2] + product[2:4] + product[4:6]


def silu(field):
    half = 0.5 * field
    return half + half * jnp.tanh(half)


def kernel(
    x_hbm, ws_hbm, wt_hbm, gain1, shift1, gain2, shift2, bias, starts, counts, out_ref,
    xv, xf, rows_m, rows_r, hrow_m, hrow_r, hcol, stat, stats, planes, acc, ws, wt, mixed,
    send_m, send_r, got_m, got_r,
    x_sem, w_sem, col_ssem, col_rsem, row_ssem, row_rsem, st_ssem, st_rsem, win_ssem, win_rsem,
):
    w = lax.axis_index("win")
    t = lax.axis_index("tile")
    r = t // TCOLS
    q = t % TCOLS
    up, down, left, right = r > 0, r < TROWS - 1, q > 0, q < TCOLS - 1
    first, last = w == 0, w == WINDOWS - 1

    x_copies = [
        pltpu.make_async_copy(x_hbm.at[:, c], xv.at[c], x_sem.at[c]) for c in range(COLS)
    ]
    for copy in x_copies:
        copy.start()
    ws_copy = pltpu.make_async_copy(ws_hbm, ws, w_sem.at[0])
    wt_copy = pltpu.make_async_copy(wt_hbm, wt, w_sem.at[1])
    ws_copy.start()
    wt_copy.start()

    barrier = pltpu.get_barrier_semaphore()
    peers = [(w, (t + i) % TILES) for i in range(1, TILES)]
    for peer in peers:
        pl.semaphore_signal(barrier, inc=1, device_id=peer, device_id_type=MESH)

    @pl.when(jnp.logical_not(first))
    def _():
        pl.semaphore_signal(barrier, inc=1, device_id=(w - 1, t), device_id_type=MESH)

    @pl.when(jnp.logical_not(last))
    def _():
        pl.semaphore_signal(barrier, inc=1, device_id=(w + 1, t), device_id_type=MESH)

    per = C // GROUPS
    group_of = lax.broadcasted_iota(jnp.int32, (C, 128), 0) // per
    to_groups = (group_of == lax.broadcasted_iota(jnp.int32, (C, 128), 1)).astype(F32).astype(BF16)
    channel_group = lax.broadcasted_iota(jnp.int32, (128, C), 1) // per
    to_channels = (
        (channel_group == lax.broadcasted_iota(jnp.int32, (128, C), 0)).astype(F32).astype(BF16)
    )

    for copy in x_copies:
        copy.wait()
    total = jnp.zeros((1, C), F32)
    square = jnp.zeros((1, C), F32)
    split = jnp.transpose(xv[...].reshape(PIX, 2, C).astype(F32), (1, 0, 2))
    for y in range(2):
        plane = split[y]
        xf[y] = plane
        rows_m[y] = plane[:, :HALF].astype(BF16)
        rows_r[y] = pack_rest(plane).astype(BF16)
        total = total + jnp.sum(plane, axis=0, keepdims=True)
        square = square + jnp.sum(plane * plane, axis=0, keepdims=True)
    stat[0] = exact_dot(jnp.concatenate([total, square], axis=0), to_groups)

    pl.semaphore_wait(
        barrier, TILES - 1 + jnp.where(first, 0, 1) + jnp.where(last, 0, 1)
    )

    def remote(src, dst, ssem, rsem, device):
        return pltpu.make_async_remote_copy(
            src_ref=src, dst_ref=dst, send_sem=ssem, recv_sem=rsem,
            device_id=device, device_id_type=MESH,
        )

    def stat_copies(which):
        return [
            remote(stat.at[which], stats.at[which, i], st_ssem.at[which, i], st_rsem.at[which, i], peers[i])
            for i in range(TILES - 1)
        ]

    first_stats = stat_copies(0)
    for copy in first_stats:
        copy.start()

    lefts, rights = xv.at[0], xv.at[COLS - 1]
    col_plan = [
        (right, rights, 1, left),
        (left, lefts, -1, right),
        (right & down, rights, TCOLS + 1, left & up),
        (left & down, lefts, TCOLS - 1, right & up),
        (right & up, rights, 1 - TCOLS, left & down),
        (left & up, lefts, -1 - TCOLS, right & down),
    ]
    col_copies = [
        remote(src, hcol.at[i], col_ssem.at[i], col_rsem.at[i], (w, (t + by + TILES) % TILES))
        for i, (_, src, by, _) in enumerate(col_plan)
    ]
    row_plan = [(down, 1, TCOLS, up), (up, 0, -TCOLS, down)]
    row_copies = [
        (
            remote(rows_m.at[y], hrow_m.at[i], row_ssem.at[i, 0], row_rsem.at[i, 0], (w, (t + by + TILES) % TILES)),
            remote(rows_r.at[y], hrow_r.at[i], row_ssem.at[i, 1], row_rsem.at[i, 1], (w, (t + by + TILES) % TILES)),
        )
        for i, (_, y, by, _) in enumerate(row_plan)
    ]

    def guarded(condition, *actions):
        @pl.when(condition)
        def _():
            for action in actions:
                action()

    for (sends, _, _, _), copy in zip(col_plan, col_copies):
        guarded(sends, copy.start)
    for (sends, _, _, _), pair in zip(row_plan, row_copies):
        guarded(sends, pair[0].start, pair[1].start)

    def finish_stats(which, copies):
        for copy in copies:
            copy.wait()
        totals = stat[which]
        for i in range(TILES - 1):
            totals = totals + stats[which, i]
        mean = totals[0:1] / MEMBERS
        spread = totals[1:2] / MEMBERS - mean * mean
        inverse = lax.rsqrt(spread + EPSILON)
        spread_out = exact_dot(jnp.concatenate([mean, inverse], axis=0), to_channels)
        return spread_out[0:1], spread_out[1:2]

    mean1, inverse1 = finish_stats(0, first_stats)
    scale1 = inverse1 * gain1[...]
    offset1 = shift1[...]

    def act(field):
        return silu((field - mean1) * scale1 + offset1).astype(BF16)

    for y in range(2):
        planes[1 + y, FRAMES : FRAMES + PIX] = act(xf[y])

    empty = jnp.zeros((FRAMES, C), BF16)
    places = [0, FRAMES * (COLS + 1)]
    for i in range(2):
        guarded(col_plan[i][3], col_copies[i].wait_recv)
        at = places[i]

        @pl.when(col_plan[i][3])
        def _(i=i, at=at):
            both = jnp.transpose(hcol[i].astype(F32), (1, 0, 2))
            for y in range(2):
                planes[1 + y, at : at + FRAMES] = act(both[y])

        @pl.when(jnp.logical_not(col_plan[i][3]))
        def _(at=at):
            for y in range(2):
                planes[1 + y, at : at + FRAMES] = empty

    for i in range(2, 6):
        guarded(col_plan[i][3], col_copies[i].wait_recv)
        at = places[i % 2]
        plane, y = (0, 1) if i < 4 else (3, 0)

        @pl.when(col_plan[i][3])
        def _(i=i, at=at, plane=plane, y=y):
            both = jnp.transpose(hcol[i].astype(F32), (1, 0, 2))
            planes[plane, at : at + FRAMES] = act(both[y])

        @pl.when(jnp.logical_not(col_plan[i][3]))
        def _(at=at, plane=plane):
            planes[plane, at : at + FRAMES] = empty

    ws_copy.wait()

    def taps(y, rows):
        summed = None
        for a in rows:
            for b in range(3):
                piece = planes[y + a, FRAMES * b : FRAMES * b + PIX]
                product = jnp.dot(piece, ws[a, b], preferred_element_type=F32)
                summed = product if summed is None else summed + product
        return summed

    acc[0] = taps(0, (1, 2))
    acc[1] = taps(1, (0, 1))

    for i in range(2):
        plane = 0 if i == 0 else 3

        @pl.when(row_plan[i][3])
        def _(i=i, plane=plane):
            row_copies[i][0].wait_recv()
            row_copies[i][1].wait_recv()
            arrived = jnp.concatenate(
                [hrow_m[i].astype(F32), unpack_rest(hrow_r[i].astype(F32))], axis=1
            )
            planes[plane, FRAMES : FRAMES + PIX] = act(arrived)

        @pl.when(jnp.logical_not(row_plan[i][3]))
        def _(plane=plane):
            planes[plane, FRAMES : FRAMES + PIX] = jnp.zeros((PIX, C), BF16)

    total = jnp.zeros((1, C), F32)
    square = jnp.zeros((1, C), F32)
    for y in range(2):
        spatial = (acc[y] + taps(y, (2 * y,))).astype(BF16).astype(F32)
        acc[y] = spatial
        total = total + jnp.sum(spatial, axis=0, keepdims=True)
        square = square + jnp.sum(spatial * spatial, axis=0, keepdims=True)
    stat[1] = exact_dot(jnp.concatenate([total, square], axis=0), to_groups)
    second_stats = stat_copies(1)
    for copy in second_stats:
        copy.start()

    lane_window = lax.broadcasted_iota(jnp.int32, (FRAMES, WINDOWS), 1)
    held = counts[...]

    def counts_of(index):
        return jnp.sum(jnp.where(lane_window == index, held, 0), axis=1, keepdims=True)

    start_lane = lax.broadcasted_iota(jnp.int32, (1, WINDOWS), 1)

    def start_of(index):
        return jnp.sum(jnp.where(start_lane == index, starts[...], 0), axis=1, keepdims=True)

    side = COLS * 2 // 5
    lane = lax.broadcasted_iota(jnp.int32, (side * FRAMES, side * FRAMES), 1)
    row = lax.broadcasted_iota(jnp.int32, (side * FRAMES, side * FRAMES), 0)
    frame = row % FRAMES
    from_prev = lane < side * SHARED
    slot = lane % SHARED
    same = row // FRAMES == (lane // SHARED) % side
    gap_prev = start_of(w) - start_of(w - 1)
    gap_next = start_of(w + 1) - start_of(w)
    wanted = jnp.where(from_prev, frame + gap_prev - (FRAMES - SHARED), frame - gap_next)
    exists = jnp.where(from_prev, jnp.where(first, 0, 1), jnp.where(last, 0, 1)) > 0
    lane16 = lax.broadcasted_iota(jnp.int32, (FRAMES, side * FRAMES), 1)
    frame16 = lax.broadcasted_iota(jnp.int32, (FRAMES, side * FRAMES), 0)
    prev_lanes = lane16 < side * SHARED
    at_frame = frame16 == lane16 % SHARED + jnp.where(prev_lanes, FRAMES - SHARED, 0)
    lane_counts = jnp.sum(
        jnp.where(at_frame, jnp.where(prev_lanes, counts_of(w - 1), counts_of(w + 1)), 0),
        axis=0,
        keepdims=True,
    )
    blend = jnp.where(same & exists & (slot == wanted), lane_counts, 0).astype(F32)
    own = jnp.concatenate([counts_of(w).astype(F32)] * side, axis=0)
    denominator = own + jnp.sum(blend, axis=1, keepdims=True)
    blend_matrix = blend.astype(BF16)

    mean2, inverse2 = finish_stats(1, second_stats)
    scale2 = inverse2 * gain2[...]
    offset2 = shift2[...]
    for y in range(2):
        mixed[y * PIX : (y + 1) * PIX] = silu((acc[y] - mean2) * scale2 + offset2).astype(BF16)

    wt_copy.wait()
    frame_at = lax.broadcasted_iota(jnp.int32, (PIX, 1), 0) % FRAMES
    blocks = []
    for y in range(2):
        piece = mixed[y * PIX : (y + 1) * PIX]
        running = xf[y] + bias[...] + jnp.dot(piece, wt[1], preferred_element_type=F32)
        before = jnp.dot(piece, wt[0], preferred_element_type=F32)
        running = running + jnp.where(frame_at > 0, pltpu.roll(before, 1, 0), 0.0)
        after = jnp.dot(piece, wt[2], preferred_element_type=F32)
        running = running + jnp.where(frame_at < FRAMES - 1, pltpu.roll(after, PIX - 1, 0), 0.0)
        block = running.astype(BF16).astype(F32)
        acc[y] = block
        halves = block.reshape(COLS, 2, SHARED, C)
        for part in range(2):
            dense = halves[:, part].reshape(COLS * SHARED, C)
            send_m[part, y * COLS * SHARED : (y + 1) * COLS * SHARED] = dense[:, :HALF].astype(BF16)
            half = COLS * SHARED // 2
            send_r[part, y * half : (y + 1) * half] = pack_rest(dense).astype(BF16)

    head = (
        remote(send_m.at[0], got_m.at[1], win_ssem.at[0, 0], win_rsem.at[0, 0], (lax.max(w - 1, 0), t)),
        remote(send_r.at[0], got_r.at[1], win_ssem.at[0, 1], win_rsem.at[0, 1], (lax.max(w - 1, 0), t)),
    )
    tail = (
        remote(send_m.at[1], got_m.at[0], win_ssem.at[1, 0], win_rsem.at[1, 0], (lax.min(w + 1, WINDOWS - 1), t)),
        remote(send_r.at[1], got_r.at[0], win_ssem.at[1, 1], win_rsem.at[1, 1], (lax.min(w + 1, WINDOWS - 1), t)),
    )
    has_prev, has_next = jnp.logical_not(first), jnp.logical_not(last)
    guarded(has_prev, head[0].start, head[1].start)
    guarded(has_next, tail[0].start, tail[1].start)

    @pl.when(first)
    def _():
        got_m[0] = jnp.zeros((PIX, HALF), BF16)
        got_r[0] = jnp.zeros((PIX // 2, 128), BF16)

    @pl.when(last)
    def _():
        got_m[1] = jnp.zeros((PIX, HALF), BF16)
        got_r[1] = jnp.zeros((PIX // 2, 128), BF16)

    for (sends, _, _, _), copy in zip(col_plan, col_copies):
        guarded(sends, copy.wait_send)
    for (sends, _, _, _), pair in zip(row_plan, row_copies):
        guarded(sends, pair[0].wait_send, pair[1].wait_send)
    guarded(has_prev, tail[0].wait_recv, tail[1].wait_recv)
    guarded(has_next, head[0].wait_recv, head[1].wait_recv)
    guarded(has_prev, head[0].wait_send, head[1].wait_send)
    guarded(has_next, tail[0].wait_send, tail[1].wait_send)

    share = 1.0 / denominator
    depth = side * SHARED
    half = COLS * SHARED // 2

    def whole(part):
        rests = [unpack_rest(got_r[part, y * half : (y + 1) * half].astype(F32)) for y in range(2)]
        rest = jnp.concatenate(rests, axis=0).astype(BF16)
        return jnp.concatenate([got_m[part], rest], axis=1)

    prev_all, next_all = whole(0), whole(1)
    own_all = acc[...].reshape(2 * PIX, C)
    joined = []
    for k in range(5):
        others = jnp.concatenate(
            [prev_all[k * depth : (k + 1) * depth], next_all[k * depth : (k + 1) * depth]], axis=0
        )
        numerator = jnp.dot(blend_matrix, others, preferred_element_type=F32)
        numerator = numerator + own * own_all[k * side * FRAMES : (k + 1) * side * FRAMES]
        joined.append(numerator * share)
    result = jnp.concatenate(joined, axis=0).reshape(2, PIX, C)
    both = jnp.stack([result[0], result[1]], axis=1).astype(BF16)
    out_ref[...] = both.reshape(COLS, FRAMES, 2, C)


def on_device(
    latents, spatial_weight, temporal_weight, gain_first, shift_first, gain_second, shift_second,
    temporal_bias, starts, blend_counts,
):
    x = jnp.transpose(latents.reshape(FRAMES, 2, COLS, C), (0, 2, 1, 3))
    vmem = pl.BlockSpec(memory_space=pltpu.VMEM)
    hbm = pl.BlockSpec(memory_space=pl.ANY)
    dma = pltpu.SemaphoreType.DMA
    out = pl.pallas_call(
        kernel,
        out_shape=jax.ShapeDtypeStruct((COLS, FRAMES, 2, C), BF16),
        in_specs=[hbm] * 3 + [vmem] * 7,
        out_specs=vmem,
        scratch_shapes=[
            pltpu.VMEM((COLS, FRAMES, 2, C), BF16),
            pltpu.VMEM((2, PIX, C), F32),
            pltpu.VMEM((2, PIX, HALF), BF16),
            pltpu.VMEM((2, PIX // 2, 128), BF16),
            pltpu.VMEM((2, PIX, HALF), BF16),
            pltpu.VMEM((2, PIX // 2, 128), BF16),
            pltpu.VMEM((6, FRAMES, 2, C), BF16),
            pltpu.VMEM((2, 2, 128), F32),
            pltpu.VMEM((2, TILES - 1, 2, 128), F32),
            pltpu.VMEM((4, WIDE, C), BF16),
            pltpu.VMEM((2, PIX, C), F32),
            pltpu.VMEM((3, 3, C, C), BF16),
            pltpu.VMEM((3, C, C), BF16),
            pltpu.VMEM((2 * PIX, C), BF16),
            pltpu.VMEM((2, PIX, HALF), BF16),
            pltpu.VMEM((2, PIX // 2, 128), BF16),
            pltpu.VMEM((2, PIX, HALF), BF16),
            pltpu.VMEM((2, PIX // 2, 128), BF16),
            dma((COLS,)),
            dma((2,)),
            dma((6,)),
            dma((6,)),
            dma((2, 2)),
            dma((2, 2)),
            dma((2, TILES - 1)),
            dma((2, TILES - 1)),
            dma((2, 2)),
            dma((2, 2)),
        ],
        compiler_params=pltpu.CompilerParams(
            collective_id=0, has_side_effects=True, vmem_limit_bytes=48 << 20
        ),
        cost_estimate=pl.CostEstimate(flops=1_600_000_000, bytes_accessed=4_000_000, transcendentals=400_000),
        name="resblock",
    )(
        x, spatial_weight, temporal_weight, gain_first.reshape(1, C), shift_first.reshape(1, C),
        gain_second.reshape(1, C), shift_second.reshape(1, C), temporal_bias.reshape(1, C),
        starts.reshape(1, WINDOWS), blend_counts.T,
    )
    return jnp.transpose(out, (1, 2, 0, 3)).reshape(1, FRAMES, 1, 2, COLS, C)


def solution(mesh):
    return jax.shard_map(
        on_device,
        mesh=mesh,
        in_specs=(P("win", None, "tile", None, None, None),) + (P(),) * 9,
        out_specs=P("win", None, "tile", None, None, None),
        check_vma=False,
    )
```

```python
import jax
import jax.numpy as jnp
from jax import lax
from jax.experimental import pallas as pl
from jax.experimental.pallas import tpu as pltpu
from jax.sharding import PartitionSpec as P

MESH = pl.DeviceIdType.MESH
F32 = jnp.float32
BF16 = jnp.bfloat16

GROUPS = 32
EPSILON = 1e-05
FRAMES = 16
SHARED = 8
TCOLS = 4
TROWS = 4
TILES = TCOLS * TROWS
WINDOWS = 32
COLS = 20
C = 320
LANES = 128
PIX = COLS * FRAMES
WIDE = (COLS + 2) * FRAMES
PACKED = PIX * 5 // 2
SIDE = 8
FIRST = 2 * SIDE * SHARED
SECOND = 3 * SIDE * SHARED
MEMBERS = float(FRAMES * TILES * 2 * COLS * (C // GROUPS))


def pack(field):
    half = field.shape[0] // 2
    rest = jnp.concatenate([field[:half, 2 * LANES :], field[half:, 2 * LANES :]], axis=1)
    return jnp.concatenate([field[:, :LANES], field[:, LANES : 2 * LANES], rest], axis=0)


def unpack(packed):
    n = packed.shape[0] * 2 // 5
    rest = packed[2 * n :]
    tail = C - 2 * LANES
    rest = jnp.concatenate([rest[:, :tail], rest[:, tail:]], axis=0)
    return jnp.concatenate([packed[:n], packed[n : 2 * n], rest], axis=1)


def exact_dot(rows, ones):
    high = rows.astype(BF16).astype(F32)
    rest = rows - high
    middle = rest.astype(BF16).astype(F32)
    low = rest - middle
    parts = jnp.concatenate([high, middle, low, jnp.zeros_like(low)], axis=0)
    product = jnp.dot(parts.astype(BF16), ones, preferred_element_type=F32)
    return product[0:2] + product[2:4] + product[4:6]


def silu(field):
    half = 0.5 * field
    return half + half * jnp.tanh(half)


def kernel(
    x_hbm, ws_hbm, wt_hbm, gain1_hbm, shift1_hbm, gain2_hbm, shift2_hbm, bias_hbm, starts_hbm, counts_hbm, out_ref,
    xv, xf, rows, hrow, hcol, stat, stats, planes, acc, ws, wt, mixed,
    send_a, send_b, got_a, got_b, passing,
    gain1, shift1, gain2, shift2, bias, starts, counts, x_sem, w_sem, small_sem, col_ssem, col_rsem, row_ssem, row_rsem, st_ssem, st_rsem, win_ssem, win_rsem, pass_ssem, pass_rsem,
):
    w = lax.axis_index("win")
    t = lax.axis_index("tile")
    r = t // TCOLS
    q = t % TCOLS
    up, down, left, right = r > 0, r < TROWS - 1, q > 0, q < TCOLS - 1
    first, last = w == 0, w == WINDOWS - 1
    x = w % 4
    has_prev, has_next = w > 0, w < WINDOWS - 1
    far_next = (x == 3) & has_next
    far_prev = (x == 0) & has_prev
    relay_up = (x == 2) & (w + 2 < WINDOWS)
    relay_down = (x == 1) & (w - 2 >= 0)

    x_copies = [
        pltpu.make_async_copy(x_hbm.at[:, c], xv.at[c], x_sem.at[c]) for c in range(COLS)
    ]
    for copy in x_copies:
        copy.start()
    ws_copy = pltpu.make_async_copy(ws_hbm, ws, w_sem.at[0])
    wt_copy = pltpu.make_async_copy(wt_hbm, wt, w_sem.at[1])
    ws_copy.start()
    wt_copy.start()

    small = [(gain1_hbm, gain1), (shift1_hbm, shift1), (gain2_hbm, gain2), (shift2_hbm, shift2),
             (bias_hbm, bias), (starts_hbm, starts), (counts_hbm, counts)]
    small_copies = [
        pltpu.make_async_copy(src, dst, small_sem.at[i]) for i, (src, dst) in enumerate(small)
    ]
    for copy in small_copies:
        copy.start()

    barrier = pltpu.get_barrier_semaphore()
    peers = [(w, (t + i) % TILES) for i in range(1, TILES)]
    for peer in peers:
        pl.semaphore_signal(barrier, inc=1, device_id=peer, device_id_type=MESH)

    greets = [
        (has_prev, w - 1),
        (has_next, w + 1),
        (relay_up | far_next, w + 2),
        (relay_down | far_prev, w - 2),
    ]
    for condition, other in greets:

        @pl.when(condition)
        def _(other=other):
            pl.semaphore_signal(barrier, inc=1, device_id=(other, t), device_id_type=MESH)

    per = C // GROUPS
    group_of = lax.broadcasted_iota(jnp.int32, (C, 128), 0) // per
    to_groups = (group_of == lax.broadcasted_iota(jnp.int32, (C, 128), 1)).astype(F32).astype(BF16)
    channel_group = lax.broadcasted_iota(jnp.int32, (128, C), 1) // per
    to_channels = (
        (channel_group == lax.broadcasted_iota(jnp.int32, (128, C), 0)).astype(F32).astype(BF16)
    )

    for copy in x_copies:
        copy.wait()
    total = jnp.zeros((1, C), F32)
    square = jnp.zeros((1, C), F32)
    split = jnp.transpose(xv[...].reshape(PIX, 2, C).astype(F32), (1, 0, 2))
    for y in range(2):
        plane = split[y]
        xf[y] = plane
        rows[y] = pack(plane).astype(BF16)
        total = total + jnp.sum(plane, axis=0, keepdims=True)
        square = square + jnp.sum(plane * plane, axis=0, keepdims=True)
    stat[0] = exact_dot(jnp.concatenate([total, square], axis=0), to_groups)

    pl.semaphore_wait(
        barrier, TILES - 1 + sum(jnp.where(condition, 1, 0) for condition, _ in greets)
    )

    def remote(src, dst, ssem, rsem, device):
        return pltpu.make_async_remote_copy(
            src_ref=src, dst_ref=dst, send_sem=ssem, recv_sem=rsem,
            device_id=device, device_id_type=MESH,
        )

    def stat_copies(which):
        return [
            remote(stat.at[which], stats.at[which, i], st_ssem.at[which, i], st_rsem.at[which, i], peers[i])
            for i in range(TILES - 1)
        ]

    first_stats = stat_copies(0)
    for copy in first_stats:
        copy.start()

    lefts, rights = xv.at[0], xv.at[COLS - 1]
    col_plan = [
        (right, rights, 1, left),
        (left, lefts, -1, right),
        (right & down, rights, TCOLS + 1, left & up),
        (left & down, lefts, TCOLS - 1, right & up),
        (right & up, rights, 1 - TCOLS, left & down),
        (left & up, lefts, -1 - TCOLS, right & down),
    ]
    col_copies = [
        remote(src, hcol.at[i], col_ssem.at[i], col_rsem.at[i], (w, (t + by + TILES) % TILES))
        for i, (_, src, by, _) in enumerate(col_plan)
    ]
    row_plan = [(down, 1, TCOLS, up), (up, 0, -TCOLS, down)]
    row_copies = [
        remote(rows.at[y], hrow.at[i], row_ssem.at[i], row_rsem.at[i], (w, (t + by + TILES) % TILES))
        for i, (_, y, by, _) in enumerate(row_plan)
    ]

    def guarded(condition, *actions):
        @pl.when(condition)
        def _():
            for action in actions:
                action()

    for (sends, _, _, _), copy in zip(col_plan, col_copies):
        guarded(sends, copy.start)
    for (sends, _, _, _), copy in zip(row_plan, row_copies):
        guarded(sends, copy.start)

    def finish_stats(which, copies):
        for copy in copies:
            copy.wait()
        totals = stat[which]
        for i in range(TILES - 1):
            totals = totals + stats[which, i]
        mean = totals[0:1] / MEMBERS
        spread = totals[1:2] / MEMBERS - mean * mean
        inverse = lax.rsqrt(spread + EPSILON)
        spread_out = exact_dot(jnp.concatenate([mean, inverse], axis=0), to_channels)
        return spread_out[0:1], spread_out[1:2]

    mean1, inverse1 = finish_stats(0, first_stats)
    for copy in small_copies:
        copy.wait()
    scale1 = inverse1 * gain1[...].reshape(1, C)
    offset1 = shift1[...].reshape(1, C)

    def act(field):
        return silu((field - mean1) * scale1 + offset1).astype(BF16)

    for y in range(2):
        planes[1 + y, FRAMES : FRAMES + PIX] = act(xf[y])

    empty = jnp.zeros((FRAMES, C), BF16)
    places = [0, FRAMES * (COLS + 1)]
    for i in range(2):
        guarded(col_plan[i][3], col_copies[i].wait_recv)
        at = places[i]

        @pl.when(col_plan[i][3])
        def _(i=i, at=at):
            both = jnp.transpose(hcol[i].astype(F32), (1, 0, 2))
            for y in range(2):
                planes[1 + y, at : at + FRAMES] = act(both[y])

        @pl.when(jnp.logical_not(col_plan[i][3]))
        def _(at=at):
            for y in range(2):
                planes[1 + y, at : at + FRAMES] = empty

    for i in range(2, 6):
        guarded(col_plan[i][3], col_copies[i].wait_recv)
        at = places[i % 2]
        plane, y = (0, 1) if i < 4 else (3, 0)

        @pl.when(col_plan[i][3])
        def _(i=i, at=at, plane=plane, y=y):
            both = jnp.transpose(hcol[i].astype(F32), (1, 0, 2))
            planes[plane, at : at + FRAMES] = act(both[y])

        @pl.when(jnp.logical_not(col_plan[i][3]))
        def _(at=at, plane=plane):
            planes[plane, at : at + FRAMES] = empty

    ws_copy.wait()

    def taps(y, rows):
        summed = None
        for a in rows:
            for b in range(3):
                piece = planes[y + a, FRAMES * b : FRAMES * b + PIX]
                product = jnp.dot(piece, ws[a, b], preferred_element_type=F32)
                summed = product if summed is None else summed + product
        return summed

    acc[0] = taps(0, (1, 2))
    acc[1] = taps(1, (0, 1))

    for i in range(2):
        plane = 0 if i == 0 else 3

        @pl.when(row_plan[i][3])
        def _(i=i, plane=plane):
            row_copies[i].wait_recv()
            planes[plane, FRAMES : FRAMES + PIX] = act(unpack(hrow[i].astype(F32)))

        @pl.when(jnp.logical_not(row_plan[i][3]))
        def _(plane=plane):
            planes[plane, FRAMES : FRAMES + PIX] = jnp.zeros((PIX, C), BF16)

    total = jnp.zeros((1, C), F32)
    square = jnp.zeros((1, C), F32)
    for y in range(2):
        spatial = (acc[y] + taps(y, (2 * y,))).astype(BF16).astype(F32)
        acc[y] = spatial
        total = total + jnp.sum(spatial, axis=0, keepdims=True)
        square = square + jnp.sum(spatial * spatial, axis=0, keepdims=True)
    stat[1] = exact_dot(jnp.concatenate([total, square], axis=0), to_groups)
    second_stats = stat_copies(1)
    for copy in second_stats:
        copy.start()

    lane_window = lax.broadcasted_iota(jnp.int32, (FRAMES, WINDOWS), 1)
    held = counts[...]

    def counts_of(index):
        return jnp.sum(jnp.where(lane_window == index, held, 0), axis=1, keepdims=True)

    start_lane = lax.broadcasted_iota(jnp.int32, (1, WINDOWS), 1)

    def start_of(index):
        return jnp.sum(jnp.where(start_lane == index, starts[...].reshape(1, WINDOWS), 0), axis=1, keepdims=True)

    side = SIDE
    lane = lax.broadcasted_iota(jnp.int32, (side * FRAMES, side * FRAMES), 1)
    row = lax.broadcasted_iota(jnp.int32, (side * FRAMES, side * FRAMES), 0)
    frame = row % FRAMES
    from_prev = lane < side * SHARED
    slot = lane % SHARED
    same = row // FRAMES == (lane // SHARED) % side
    gap_prev = start_of(w) - start_of(w - 1)
    gap_next = start_of(w + 1) - start_of(w)
    wanted = jnp.where(from_prev, frame + gap_prev - (FRAMES - SHARED), frame - gap_next)
    exists = jnp.where(from_prev, jnp.where(first, 0, 1), jnp.where(last, 0, 1)) > 0
    lane16 = lax.broadcasted_iota(jnp.int32, (FRAMES, side * FRAMES), 1)
    frame16 = lax.broadcasted_iota(jnp.int32, (FRAMES, side * FRAMES), 0)
    prev_lanes = lane16 < side * SHARED
    at_frame = frame16 == lane16 % SHARED + jnp.where(prev_lanes, FRAMES - SHARED, 0)
    lane_counts = jnp.sum(
        jnp.where(at_frame, jnp.where(prev_lanes, counts_of(w - 1), counts_of(w + 1)), 0),
        axis=0,
        keepdims=True,
    )
    blend = jnp.where(same & exists & (slot == wanted), lane_counts, 0).astype(F32)
    own = jnp.concatenate([counts_of(w).astype(F32)] * side, axis=0)
    denominator = own + jnp.sum(blend, axis=1, keepdims=True)
    blend_matrix = blend.astype(BF16)

    mean2, inverse2 = finish_stats(1, second_stats)
    scale2 = inverse2 * gain2[...].reshape(1, C)
    offset2 = shift2[...].reshape(1, C)
    for y in range(2):
        mixed[y * PIX : (y + 1) * PIX] = silu((acc[y] - mean2) * scale2 + offset2).astype(BF16)

    wt_copy.wait()
    frame_at = lax.broadcasted_iota(jnp.int32, (PIX, 1), 0) % FRAMES
    def window(index):
        return (lax.clamp(0, index, WINDOWS - 1), t)

    direct_a = [
        remote(send_a.at[0], got_a.at[1], win_ssem.at[0, 0], win_rsem.at[0, 0], window(w - 1)),
        remote(send_a.at[1], got_a.at[0], win_ssem.at[1, 0], win_rsem.at[1, 0], window(w + 1)),
    ]
    direct_b = [
        remote(send_b.at[0], got_b.at[1], win_ssem.at[0, 1], win_rsem.at[0, 1], window(w - 1)),
        remote(send_b.at[1], got_b.at[0], win_ssem.at[1, 1], win_rsem.at[1, 1], window(w + 1)),
    ]
    aside = [
        remote(send_a.at[0], passing, win_ssem.at[0, 0], pass_rsem.at[0], window(w + 1)),
        remote(send_a.at[1], passing, win_ssem.at[1, 0], pass_rsem.at[0], window(w - 1)),
    ]
    onward = [
        remote(passing, got_a.at[1], pass_ssem.at[0], win_rsem.at[0, 0], window(w - 2)),
        remote(passing, got_a.at[0], pass_ssem.at[0], win_rsem.at[1, 0], window(w + 2)),
    ]

    @pl.when(first)
    def _():
        got_a[0] = jnp.zeros_like(got_a[0])
        got_b[0] = jnp.zeros_like(got_b[0])

    @pl.when(last)
    def _():
        got_a[1] = jnp.zeros_like(got_a[1])
        got_b[1] = jnp.zeros_like(got_b[1])

    frame_rows = COLS * SHARED
    left_over = []
    for y in range(2):
        piece = mixed[y * PIX : (y + 1) * PIX]
        running = xf[y] + bias[...].reshape(1, C) + jnp.dot(piece, wt[1], preferred_element_type=F32)
        before = jnp.dot(piece, wt[0], preferred_element_type=F32)
        running = running + jnp.where(frame_at > 0, pltpu.roll(before, 1, 0), 0.0)
        after = jnp.dot(piece, wt[2], preferred_element_type=F32)
        running = running + jnp.where(frame_at < FRAMES - 1, pltpu.roll(after, PIX - 1, 0), 0.0)
        block = running.astype(BF16).astype(F32)
        acc[y] = block
        halves = block.reshape(COLS, 2, SHARED, C)
        for part in range(2):
            dense = halves[:, part].reshape(frame_rows, C)
            if y == 0:
                send_a[part] = pack(dense[:FIRST]).astype(BF16)
                left_over.append(dense[FIRST:])
            else:
                send_b[part] = pack(jnp.concatenate([left_over[part], dense], axis=0)).astype(BF16)
        if y == 0:
            guarded(has_prev & jnp.logical_not(far_prev), direct_a[0].start)
            guarded(has_next & jnp.logical_not(far_next), direct_a[1].start)
            guarded(far_prev, aside[0].start)
            guarded(far_next, aside[1].start)
    guarded(has_prev, direct_b[0].start)
    guarded(has_next, direct_b[1].start)
    guarded(relay_down, aside[0].wait_recv, onward[0].start)
    guarded(relay_up, aside[1].wait_recv, onward[1].start)

    for (sends, _, _, _), copy in zip(col_plan, col_copies):
        guarded(sends, copy.wait_send)
    for (sends, _, _, _), copy in zip(row_plan, row_copies):
        guarded(sends, copy.wait_send)
    guarded(has_prev, direct_a[1].wait_recv, direct_b[1].wait_recv)
    guarded(has_next, direct_a[0].wait_recv, direct_b[0].wait_recv)
    guarded(has_prev, direct_a[0].wait_send, direct_b[0].wait_send)
    guarded(has_next, direct_a[1].wait_send, direct_b[1].wait_send)
    guarded(relay_down, onward[0].wait_send)
    guarded(relay_up, onward[1].wait_send)

    share = 1.0 / denominator
    depth = side * SHARED

    def whole(part):
        return jnp.concatenate([unpack(got_a[part]), unpack(got_b[part])], axis=0)

    prev_all, next_all = whole(0), whole(1)
    own_all = acc[...].reshape(2 * PIX, C)
    joined = []
    for k in range(5):
        others = jnp.concatenate(
            [prev_all[k * depth : (k + 1) * depth], next_all[k * depth : (k + 1) * depth]], axis=0
        )
        numerator = jnp.dot(blend_matrix, others, preferred_element_type=F32)
        numerator = numerator + own * own_all[k * side * FRAMES : (k + 1) * side * FRAMES]
        joined.append(numerator * share)
    result = jnp.concatenate(joined, axis=0).reshape(2, PIX, C)
    both = jnp.stack([result[0], result[1]], axis=1).astype(BF16)
    out_ref[...] = both.reshape(COLS, FRAMES, 2, C)


def on_device(
    latents, spatial_weight, temporal_weight, gain_first, shift_first, gain_second, shift_second,
    temporal_bias, starts, blend_counts,
):
    x = jnp.transpose(latents.reshape(FRAMES, 2, COLS, C), (0, 2, 1, 3))
    vmem = pl.BlockSpec(memory_space=pltpu.VMEM)
    hbm = pl.BlockSpec(memory_space=pltpu.HBM)
    dma = pltpu.SemaphoreType.DMA
    out = pl.pallas_call(
        kernel,
        out_shape=jax.ShapeDtypeStruct((COLS, FRAMES, 2, C), BF16),
        in_specs=[hbm] * 10,
        out_specs=vmem,
        scratch_shapes=[
            pltpu.VMEM((COLS, FRAMES, 2, C), BF16),
            pltpu.VMEM((2, PIX, C), F32),
            pltpu.VMEM((2, PACKED, LANES), BF16),
            pltpu.VMEM((2, PACKED, LANES), BF16),
            pltpu.VMEM((6, FRAMES, 2, C), BF16),
            pltpu.VMEM((2, 2, 128), F32),
            pltpu.VMEM((2, TILES - 1, 2, 128), F32),
            pltpu.VMEM((4, WIDE, C), BF16),
            pltpu.VMEM((2, PIX, C), F32),
            pltpu.VMEM((3, 3, C, C), BF16),
            pltpu.VMEM((3, C, C), BF16),
            pltpu.VMEM((2 * PIX, C), BF16),
            pltpu.VMEM((2, FIRST * 5 // 2, LANES), BF16),
            pltpu.VMEM((2, SECOND * 5 // 2, LANES), BF16),
            pltpu.VMEM((2, FIRST * 5 // 2, LANES), BF16),
            pltpu.VMEM((2, SECOND * 5 // 2, LANES), BF16),
            pltpu.VMEM((FIRST * 5 // 2, LANES), BF16),
            pltpu.VMEM((C,), F32),
            pltpu.VMEM((C,), F32),
            pltpu.VMEM((C,), F32),
            pltpu.VMEM((C,), F32),
            pltpu.VMEM((C,), F32),
            pltpu.VMEM((WINDOWS,), jnp.int32),
            pltpu.VMEM((FRAMES, WINDOWS), jnp.int32),
            dma((COLS,)),
            dma((2,)),
            dma((7,)),
            dma((6,)),
            dma((6,)),
            dma((2,)),
            dma((2,)),
            dma((2, TILES - 1)),
            dma((2, TILES - 1)),
            dma((2, 2)),
            dma((2, 2)),
            dma((1,)),
            dma((1,)),
        ],
        compiler_params=pltpu.CompilerParams(
            collective_id=0, has_side_effects=True, vmem_limit_bytes=60 << 20
        ),
        cost_estimate=pl.CostEstimate(flops=1_600_000_000, bytes_accessed=4_000_000, transcendentals=400_000),
        name="resblock",
    )(
        x, spatial_weight, temporal_weight, gain_first, shift_first, gain_second, shift_second,
        temporal_bias, starts, blend_counts.T,
    )
    return jnp.transpose(out, (1, 2, 0, 3)).reshape(1, FRAMES, 1, 2, COLS, C)


def solution(mesh):
    return jax.shard_map(
        on_device,
        mesh=mesh,
        in_specs=(P("win", None, "tile", None, None, None),) + (P(),) * 9,
        out_specs=P("win", None, "tile", None, None, None),
        check_vma=False,
    )
```

```python
import jax
import jax.numpy as jnp
from jax import lax
from jax.experimental import pallas as pl
from jax.experimental.pallas import tpu as pltpu
from jax.sharding import PartitionSpec as P

MESH = pl.DeviceIdType.MESH
F32 = jnp.float32
BF16 = jnp.bfloat16

GROUPS = 32
EPSILON = 1e-05
FRAMES = 16
SHARED = 8
TCOLS = 4
TROWS = 4
TILES = TCOLS * TROWS
WINDOWS = 32
COLS = 20
C = 320
LANES = 128
PIX = COLS * FRAMES
WIDE = (COLS + 2) * FRAMES
PACKED = PIX * 5 // 2
SIDE = 8
CHUNKS = (64, 64, 192)
PASSED = 2
STARTS = tuple(sum(CHUNKS[:i]) for i in range(len(CHUNKS) + 1))
ROW_CHUNKS = (64, 256)
ROW_STARTS = (0, 64, 320)
MEMBERS = float(FRAMES * TILES * 2 * COLS * (C // GROUPS))


def pack(field):
    half = field.shape[0] // 2
    rest = jnp.concatenate([field[:half, 2 * LANES :], field[half:, 2 * LANES :]], axis=1)
    return jnp.concatenate([field[:, :LANES], field[:, LANES : 2 * LANES], rest], axis=0)


def unpack(packed):
    n = packed.shape[0] * 2 // 5
    rest = packed[2 * n :]
    tail = C - 2 * LANES
    rest = jnp.concatenate([rest[:, :tail], rest[:, tail:]], axis=0)
    return jnp.concatenate([packed[:n], packed[n : 2 * n], rest], axis=1)


def rows_at(starts, k):
    return pl.ds(starts[k] * 5 // 2, (starts[k + 1] - starts[k]) * 5 // 2)


def joined_dot(pieces, weights):
    cut = 2 * LANES
    left = jnp.concatenate([p[:, :cut] for p in pieces] + [p[:, cut:] for p in pieces], axis=1)
    right = jnp.concatenate([m[:cut] for m in weights] + [m[cut:] for m in weights], axis=0)
    return jnp.dot(left, right, preferred_element_type=F32)


def exact_dot(rows, ones):
    high = rows.astype(BF16).astype(F32)
    rest = rows - high
    middle = rest.astype(BF16).astype(F32)
    low = rest - middle
    parts = jnp.concatenate([high, middle, low, jnp.zeros_like(low)], axis=0)
    product = jnp.dot(parts.astype(BF16), ones, preferred_element_type=F32)
    return product[0:2] + product[2:4] + product[4:6]


def silu(field):
    half = 0.5 * field
    return half + half * jnp.tanh(half)


def kernel(
    x_hbm, ws_hbm, wt_hbm, gain1_hbm, shift1_hbm, gain2_hbm, shift2_hbm, bias_hbm, starts_hbm, counts_hbm, out_hbm,
    xv, xf, rows, hrow, hcol, stat, stats, planes, acc, ws, wt, merged, out_v,
    send, got, passing,
    gain1, shift1, gain2, shift2, bias, starts, counts, x_sem, w_sem, small_sem, out_sem, near_sem, far_sem, col_ssem, col_rsem, row_ssem, row_rsem, st_ssem, st_rsem, win_ssem, win_rsem, pass_ssem, pass_rsem,
):
    w = lax.axis_index("win")
    t = lax.axis_index("tile")
    r = t // TCOLS
    q = t % TCOLS
    up, down, left, right = r > 0, r < TROWS - 1, q > 0, q < TCOLS - 1
    first, last = w == 0, w == WINDOWS - 1
    x = w % 4
    has_prev, has_next = w > 0, w < WINDOWS - 1
    far_next = (x == 3) & has_next
    far_prev = (x == 0) & has_prev
    relay_up = (x == 2) & (w + 2 < WINDOWS)
    relay_down = (x == 1) & (w - 2 >= 0)

    x_copies = [
        pltpu.make_async_copy(x_hbm.at[:, c], xv.at[c], x_sem.at[c]) for c in range(COLS)
    ]
    for copy in x_copies:
        copy.start()
    ws_copy = pltpu.make_async_copy(ws_hbm, ws, w_sem.at[0])
    wt_copy = pltpu.make_async_copy(wt_hbm, wt, w_sem.at[1])
    ws_copy.start()
    wt_copy.start()

    small = [(gain1_hbm, gain1), (shift1_hbm, shift1), (gain2_hbm, gain2), (shift2_hbm, shift2),
             (bias_hbm, bias), (starts_hbm, starts), (counts_hbm, counts)]
    small_copies = [
        pltpu.make_async_copy(src, dst, small_sem.at[i]) for i, (src, dst) in enumerate(small)
    ]
    for copy in small_copies:
        copy.start()

    barrier = pltpu.get_barrier_semaphore()
    peers = [(w, (t + i) % TILES) for i in range(1, TILES)]
    greets = [
        (has_prev, w - 1),
        (has_next, w + 1),
        (relay_up | far_next, w + 2),
        (relay_down | far_prev, w - 2),
    ]

    core, chip = t % 2, t // 2
    chips = TILES // 2
    is_near = [jnp.abs(k - chip) <= 2 for k in range(chips)]
    for k in range(chips):

        @pl.when(chip != k)
        def _(k=k):
            at = 2 * k + jnp.where(is_near[k], 1, 0)
            pl.semaphore_signal(barrier, inc=1, device_id=(w, at), device_id_type=MESH)

    @pl.when(core == 0)
    def _():
        pl.semaphore_signal(barrier, inc=1, device_id=(w, t + 1), device_id_type=MESH)

    for condition, other in greets:

        @pl.when(condition)
        def _(other=other):
            pl.semaphore_signal(barrier, inc=1, device_id=(other, t - core), device_id_type=MESH)

    near_count = 2 * sum(jnp.where(near, 1, 0) for near in is_near) - 1
    far_count = 2 * sum(jnp.where(near, 0, 1) for near in is_near) + 2 * sum(
        jnp.where(condition, 1, 0) for condition, _ in greets
    )

    per = C // GROUPS
    group_of = lax.broadcasted_iota(jnp.int32, (C, 128), 0) // per
    to_groups = (group_of == lax.broadcasted_iota(jnp.int32, (C, 128), 1)).astype(F32).astype(BF16)
    channel_group = lax.broadcasted_iota(jnp.int32, (128, C), 1) // per
    to_channels = (
        (channel_group == lax.broadcasted_iota(jnp.int32, (128, C), 0)).astype(F32).astype(BF16)
    )

    for copy in x_copies:
        copy.wait()
    total = jnp.zeros((1, C), F32)
    square = jnp.zeros((1, C), F32)
    split = jnp.transpose(xv[...].reshape(PIX, 2, C).astype(F32), (1, 0, 2))
    for y in range(2):
        plane = split[y]
        xf[y] = plane
        for k in range(len(ROW_CHUNKS)):
            part = plane[ROW_STARTS[k] : ROW_STARTS[k + 1]]
            rows[y, rows_at(ROW_STARTS, k)] = pack(part).astype(BF16)
        total = total + jnp.sum(plane, axis=0, keepdims=True)
        square = square + jnp.sum(plane * plane, axis=0, keepdims=True)

    @pl.when(core == 1)
    def _():
        pl.semaphore_wait(barrier, near_count)
        pl.semaphore_signal(near_sem, inc=1, device_id=(w, t - 1), device_id_type=MESH)

    @pl.when(core == 0)
    def _():
        pl.semaphore_wait(near_sem, 1)

    def remote(src, dst, ssem, rsem, device):
        return pltpu.make_async_remote_copy(
            src_ref=src, dst_ref=dst, send_sem=ssem, recv_sem=rsem,
            device_id=device, device_id_type=MESH,
        )

    def stat_copies(which):
        return [
            remote(stat.at[which], stats.at[which, i], st_ssem.at[which, i], st_rsem.at[which, i], peers[i])
            for i in range(TILES - 1)
        ]

    lefts, rights = xv.at[0], xv.at[COLS - 1]
    col_plan = [
        (right, rights, 1, left),
        (left, lefts, -1, right),
        (right & down, rights, TCOLS + 1, left & up),
        (left & down, lefts, TCOLS - 1, right & up),
        (right & up, rights, 1 - TCOLS, left & down),
        (left & up, lefts, -1 - TCOLS, right & down),
    ]
    col_copies = [
        remote(src, hcol.at[i], col_ssem.at[i], col_rsem.at[i], (w, (t + by + TILES) % TILES))
        for i, (_, src, by, _) in enumerate(col_plan)
    ]
    row_plan = [(down, 1, TCOLS, up), (up, 0, -TCOLS, down)]
    row_copies = [
        [
            remote(
                rows.at[y, rows_at(ROW_STARTS, k)], hrow.at[i, rows_at(ROW_STARTS, k)],
                row_ssem.at[i, k], row_rsem.at[i, k], (w, (t + by + TILES) % TILES),
            )
            for i, (_, y, by, _) in enumerate(row_plan)
        ]
        for k in range(len(ROW_CHUNKS))
    ]

    def guarded(condition, *actions):
        @pl.when(condition)
        def _():
            for action in actions:
                action()

    for i in range(2):
        guarded(row_plan[i][0], row_copies[0][i].start)

    stat[0] = exact_dot(jnp.concatenate([total, square], axis=0), to_groups)

    @pl.when(core == 0)
    def _():
        pl.semaphore_wait(barrier, far_count)
        pl.semaphore_signal(far_sem, inc=1, device_id=(w, t + 1), device_id_type=MESH)

    @pl.when(core == 1)
    def _():
        pl.semaphore_wait(far_sem, 1)

    first_stats = stat_copies(0)
    for copy in first_stats:
        copy.start()
    for i in range(6):
        guarded(col_plan[i][0], col_copies[i].start)
    for k in range(1, len(ROW_CHUNKS)):
        for i in range(2):
            guarded(row_plan[i][0], row_copies[k][i].start)

    def finish_stats(which, copies):
        for copy in copies:
            copy.wait()
        totals = stat[which]
        for i in range(TILES - 1):
            totals = totals + stats[which, i]
        mean = totals[0:1] / MEMBERS
        spread = totals[1:2] / MEMBERS - mean * mean
        inverse = lax.rsqrt(spread + EPSILON)
        spread_out = exact_dot(jnp.concatenate([mean, inverse], axis=0), to_channels)
        return spread_out[0:1], spread_out[1:2]

    mean1, inverse1 = finish_stats(0, first_stats)
    for copy in small_copies:
        copy.wait()
    scale1 = inverse1 * gain1[...].reshape(1, C)
    offset1 = shift1[...].reshape(1, C)

    def act(field):
        return silu((field - mean1) * scale1 + offset1).astype(BF16)

    for y in range(2):
        planes[1 + y, FRAMES : FRAMES + PIX] = act(xf[y])

    empty = jnp.zeros((FRAMES, C), BF16)
    places = [0, FRAMES * (COLS + 1)]
    for i in range(2):
        guarded(col_plan[i][3], col_copies[i].wait_recv)
        at = places[i]

        @pl.when(col_plan[i][3])
        def _(i=i, at=at):
            both = jnp.transpose(hcol[i].astype(F32), (1, 0, 2))
            for y in range(2):
                planes[1 + y, at : at + FRAMES] = act(both[y])

        @pl.when(jnp.logical_not(col_plan[i][3]))
        def _(at=at):
            for y in range(2):
                planes[1 + y, at : at + FRAMES] = empty

    for i in range(2, 6):
        guarded(col_plan[i][3], col_copies[i].wait_recv)
        at = places[i % 2]
        plane, y = (0, 1) if i < 4 else (3, 0)

        @pl.when(col_plan[i][3])
        def _(i=i, at=at, plane=plane, y=y):
            both = jnp.transpose(hcol[i].astype(F32), (1, 0, 2))
            planes[plane, at : at + FRAMES] = act(both[y])

        @pl.when(jnp.logical_not(col_plan[i][3]))
        def _(at=at, plane=plane):
            planes[plane, at : at + FRAMES] = empty

    ws_copy.wait()

    def taps(y, rows):
        pairs = [(a, b) for a in rows for b in range(3)]
        return joined_dot(
            [planes[y + a, FRAMES * b : FRAMES * b + PIX] for a, b in pairs], [ws[a, b] for a, b in pairs]
        )

    acc[0] = taps(0, (1, 2))
    acc[1] = taps(1, (0, 1))

    for i in range(2):
        plane = 0 if i == 0 else 3

        @pl.when(row_plan[i][3])
        def _(i=i, plane=plane):
            for k in range(len(ROW_CHUNKS)):
                row_copies[k][i].wait_recv()
                arrived = unpack(hrow[i, rows_at(ROW_STARTS, k)].astype(F32))
                planes[plane, FRAMES + ROW_STARTS[k] : FRAMES + ROW_STARTS[k + 1]] = act(arrived)

        @pl.when(jnp.logical_not(row_plan[i][3]))
        def _(plane=plane):
            planes[plane, FRAMES : FRAMES + PIX] = jnp.zeros((PIX, C), BF16)

    total = jnp.zeros((1, C), F32)
    square = jnp.zeros((1, C), F32)
    for y in range(2):
        spatial = (acc[y] + taps(y, (2 * y,))).astype(BF16).astype(F32)
        acc[y] = spatial
        total = total + jnp.sum(spatial, axis=0, keepdims=True)
        square = square + jnp.sum(spatial * spatial, axis=0, keepdims=True)
    stat[1] = exact_dot(jnp.concatenate([total, square], axis=0), to_groups)
    second_stats = stat_copies(1)
    for copy in second_stats:
        copy.start()

    lane_window = lax.broadcasted_iota(jnp.int32, (FRAMES, WINDOWS), 1)
    held = counts[...]

    def counts_of(index):
        return jnp.sum(jnp.where(lane_window == index, held, 0), axis=1, keepdims=True)

    start_lane = lax.broadcasted_iota(jnp.int32, (1, WINDOWS), 1)

    def start_of(index):
        return jnp.sum(jnp.where(start_lane == index, starts[...].reshape(1, WINDOWS), 0), axis=1, keepdims=True)

    side = SIDE
    lane = lax.broadcasted_iota(jnp.int32, (side * FRAMES, side * FRAMES), 1)
    row = lax.broadcasted_iota(jnp.int32, (side * FRAMES, side * FRAMES), 0)
    frame = row % FRAMES
    from_prev = lane < side * SHARED
    slot = lane % SHARED
    same = row // FRAMES == (lane // SHARED) % side
    gap_prev = start_of(w) - start_of(w - 1)
    gap_next = start_of(w + 1) - start_of(w)
    wanted = jnp.where(from_prev, frame + gap_prev - (FRAMES - SHARED), frame - gap_next)
    exists = jnp.where(from_prev, jnp.where(first, 0, 1), jnp.where(last, 0, 1)) > 0
    lane16 = lax.broadcasted_iota(jnp.int32, (FRAMES, side * FRAMES), 1)
    frame16 = lax.broadcasted_iota(jnp.int32, (FRAMES, side * FRAMES), 0)
    prev_lanes = lane16 < side * SHARED
    at_frame = frame16 == lane16 % SHARED + jnp.where(prev_lanes, FRAMES - SHARED, 0)
    lane_counts = jnp.sum(
        jnp.where(at_frame, jnp.where(prev_lanes, counts_of(w - 1), counts_of(w + 1)), 0),
        axis=0,
        keepdims=True,
    )
    blend = jnp.where(same & exists & (slot == wanted), lane_counts, 0).astype(F32)
    own = jnp.concatenate([counts_of(w).astype(F32)] * side, axis=0)
    denominator = own + jnp.sum(blend, axis=1, keepdims=True)
    blend_matrix = blend.astype(BF16)

    mean2, inverse2 = finish_stats(1, second_stats)
    scale2 = inverse2 * gain2[...].reshape(1, C)
    offset2 = shift2[...].reshape(1, C)

    wt_copy.wait()
    frame_at = lax.broadcasted_iota(jnp.int32, (PIX, 1), 0) % FRAMES
    def window(index):
        return (lax.clamp(0, index, WINDOWS - 1), t)

    direct, aside, onward = [], [], []
    for k in range(len(CHUNKS)):
        at = rows_at(STARTS, k)
        direct.append([
            remote(send.at[0, at], got.at[1, at], win_ssem.at[0, k], win_rsem.at[0, k], window(w - 1)),
            remote(send.at[1, at], got.at[0, at], win_ssem.at[1, k], win_rsem.at[1, k], window(w + 1)),
        ])
        if k < PASSED:
            aside.append([
                remote(send.at[0, at], passing.at[at], win_ssem.at[0, k], pass_rsem.at[k], window(w + 1)),
                remote(send.at[1, at], passing.at[at], win_ssem.at[1, k], pass_rsem.at[k], window(w - 1)),
            ])
            onward.append([
                remote(passing.at[at], got.at[1, at], pass_ssem.at[k], win_rsem.at[0, k], window(w - 2)),
                remote(passing.at[at], got.at[0, at], pass_ssem.at[k], win_rsem.at[1, k], window(w + 2)),
            ])

    def send_chunk(k):
        if k < PASSED:
            guarded(has_prev & jnp.logical_not(far_prev), direct[k][0].start)
            guarded(has_next & jnp.logical_not(far_next), direct[k][1].start)
            guarded(far_prev, aside[k][0].start)
            guarded(far_next, aside[k][1].start)
        else:
            guarded(has_prev, direct[k][0].start)
            guarded(has_next, direct[k][1].start)

    @pl.when(first)
    def _():
        got[0] = jnp.zeros_like(got[0])

    @pl.when(last)
    def _():
        got[1] = jnp.zeros_like(got[1])

    frame_rows = COLS * SHARED
    left_over, done = None, 0
    for y in range(2):
        mixed = silu((acc[y] - mean2) * scale2 + offset2)
        before = jnp.where(frame_at > 0, pltpu.roll(mixed, 1, 0), 0.0)
        after = jnp.where(frame_at < FRAMES - 1, pltpu.roll(mixed, PIX - 1, 0), 0.0)
        running = xf[y] + bias[...].reshape(1, C) + joined_dot(
            [before.astype(BF16), mixed.astype(BF16), after.astype(BF16)], [wt[k] for k in range(3)]
        )
        block = running.astype(BF16).astype(F32)
        acc[y] = block
        halves = block.reshape(COLS, 2, SHARED, C)
        dense = [halves[:, part].reshape(frame_rows, C) for part in range(2)]
        if left_over is not None:
            dense = [jnp.concatenate([left_over[part], dense[part]], axis=0) for part in range(2)]
        base = 0 if y == 0 else STARTS[done]
        for k in range(done, len(CHUNKS)):
            if STARTS[k + 1] > frame_rows * (y + 1):
                break
            for part in range(2):
                chunk = dense[part][STARTS[k] - base : STARTS[k + 1] - base]
                send[part, rows_at(STARTS, k)] = pack(chunk).astype(BF16)
            send_chunk(k)
            done = k + 1
        if STARTS[done] < frame_rows * (y + 1):
            left_over = [dense[part][STARTS[done] - base :] for part in range(2)]
        else:
            left_over = None
    for k in range(PASSED):
        guarded(relay_down, aside[k][0].wait_recv, onward[k][0].start)
        guarded(relay_up, aside[k][1].wait_recv, onward[k][1].start)

    for (sends, _, _, _), copy in zip(col_plan, col_copies):
        guarded(sends, copy.wait_send)
    for k in range(len(ROW_CHUNKS)):
        for i in range(2):
            guarded(row_plan[i][0], row_copies[k][i].wait_send)
    for k in range(len(CHUNKS)):
        guarded(has_prev, direct[k][1].wait_recv, direct[k][0].wait_send)
        guarded(has_next, direct[k][0].wait_recv, direct[k][1].wait_send)
    for k in range(PASSED):
        guarded(relay_down, onward[k][0].wait_send)
        guarded(relay_up, onward[k][1].wait_send)

    share = 1.0 / denominator
    depth = side * SHARED

    def whole(part):
        return jnp.concatenate([unpack(got[part, rows_at(STARTS, k)]) for k in range(len(CHUNKS))], axis=0)

    prev_all, next_all = whole(0), whole(1)
    own_all = acc[...].reshape(2 * PIX, C)
    height = side * FRAMES
    out_copies = [
        pltpu.make_async_copy(out_v.at[c], out_hbm.at[:, c], out_sem.at[c]) for c in range(COLS)
    ]
    written = 0
    for k in range(5):
        others = jnp.concatenate(
            [prev_all[k * depth : (k + 1) * depth], next_all[k * depth : (k + 1) * depth]], axis=0
        )
        numerator = jnp.dot(blend_matrix, others, preferred_element_type=F32)
        numerator = numerator + own * own_all[k * height : (k + 1) * height]
        result = numerator * share
        for y in range(2):
            low = max(k * height, y * PIX)
            high = min((k + 1) * height, (y + 1) * PIX)
            if low >= high:
                continue
            part = result[low - k * height : high - k * height]
            at = pl.ds(2 * (low - y * PIX) + y, high - low, stride=2)
            for n in range(2):
                merged[n, at, :] = part[:, n * LANES : (n + 1) * LANES]
            merged[2, at, : C - 2 * LANES] = part[:, 2 * LANES :]
        ready = max(0, (k + 1) * side - COLS)
        if ready > written:
            for n in range(3):
                wide = min(LANES, C - n * LANES)
                piece = merged[n, 2 * FRAMES * written : 2 * FRAMES * ready, :wide].astype(BF16)
                out_v[written:ready, :, :, n * LANES : n * LANES + wide] = piece.reshape(
                    ready - written, FRAMES, 2, wide
                )
            for c in range(written, ready):
                out_copies[c].start()
            written = ready
    for copy in out_copies:
        copy.wait()


def on_device(
    latents, spatial_weight, temporal_weight, gain_first, shift_first, gain_second, shift_second,
    temporal_bias, starts, blend_counts,
):
    x = jnp.transpose(latents.reshape(FRAMES, 2, COLS, C), (0, 2, 1, 3))
    hbm = pl.BlockSpec(memory_space=pltpu.HBM)
    dma = pltpu.SemaphoreType.DMA
    out = pl.pallas_call(
        kernel,
        out_shape=jax.ShapeDtypeStruct((FRAMES, COLS, 2, C), BF16),
        in_specs=[hbm] * 10,
        out_specs=hbm,
        scratch_shapes=[
            pltpu.VMEM((COLS, FRAMES, 2, C), BF16),
            pltpu.VMEM((2, PIX, C), F32),
            pltpu.VMEM((2, PACKED, LANES), BF16),
            pltpu.VMEM((2, PACKED, LANES), BF16),
            pltpu.VMEM((6, FRAMES, 2, C), BF16),
            pltpu.VMEM((2, 2, 128), F32),
            pltpu.VMEM((2, TILES - 1, 2, 128), F32),
            pltpu.VMEM((4, WIDE, C), BF16),
            pltpu.VMEM((2, PIX, C), F32),
            pltpu.VMEM((3, 3, C, C), BF16),
            pltpu.VMEM((3, C, C), BF16),
            pltpu.VMEM((3, 2 * PIX, LANES), F32),
            pltpu.VMEM((COLS, FRAMES, 2, C), BF16),
            pltpu.VMEM((2, PACKED, LANES), BF16),
            pltpu.VMEM((2, PACKED, LANES), BF16),
            pltpu.VMEM((STARTS[PASSED] * 5 // 2, LANES), BF16),
            pltpu.VMEM((C,), F32),
            pltpu.VMEM((C,), F32),
            pltpu.VMEM((C,), F32),
            pltpu.VMEM((C,), F32),
            pltpu.VMEM((C,), F32),
            pltpu.VMEM((WINDOWS,), jnp.int32),
            pltpu.VMEM((FRAMES, WINDOWS), jnp.int32),
            dma((COLS,)),
            dma((2,)),
            dma((7,)),
            dma((COLS,)),
            pltpu.SemaphoreType.REGULAR,
            pltpu.SemaphoreType.REGULAR,
            dma((6,)),
            dma((6,)),
            dma((2, len(ROW_CHUNKS))),
            dma((2, len(ROW_CHUNKS))),
            dma((2, TILES - 1)),
            dma((2, TILES - 1)),
            dma((2, len(CHUNKS))),
            dma((2, len(CHUNKS))),
            dma((PASSED,)),
            dma((PASSED,)),
        ],
        compiler_params=pltpu.CompilerParams(
            collective_id=0, has_side_effects=True, vmem_limit_bytes=60 << 20
        ),
        cost_estimate=pl.CostEstimate(flops=1_600_000_000, bytes_accessed=4_000_000, transcendentals=400_000),
        name="resblock",
    )(
        x, spatial_weight, temporal_weight, gain_first, shift_first, gain_second, shift_second,
        temporal_bias, starts, blend_counts.T,
    )
    return jnp.transpose(out, (0, 2, 1, 3)).reshape(1, FRAMES, 1, 2, COLS, C)


def solution(mesh):
    return jax.shard_map(
        on_device,
        mesh=mesh,
        in_specs=(P("win", None, "tile", None, None, None),) + (P(),) * 9,
        out_specs=P("win", None, "tile", None, None, None),
        check_vma=False,
    )
```

```python
import jax
import jax.numpy as jnp
from jax import lax
from jax.experimental import pallas as pl
from jax.experimental.pallas import tpu as pltpu
from jax.sharding import PartitionSpec as P

MESH = pl.DeviceIdType.MESH
F32 = jnp.float32
BF16 = jnp.bfloat16

GROUPS = 32
EPSILON = 1e-05
FRAMES = 16
SHARED = 8
TCOLS = 4
TROWS = 4
TILES = TCOLS * TROWS
WINDOWS = 32
COLS = 20
C = 320
LANES = 128
PIX = COLS * FRAMES
WIDE = (COLS + 2) * FRAMES
PACKED = PIX * 5 // 2
SIDE = 8
CHUNKS = (64, 64, 32, 160)
PASSED = 2
STARTS = tuple(sum(CHUNKS[:i]) for i in range(len(CHUNKS) + 1))
ROW_CHUNKS = (64, 256)
ROW_STARTS = (0, 64, 320)
MEMBERS = float(FRAMES * TILES * 2 * COLS * (C // GROUPS))


def pack(field):
    half = field.shape[0] // 2
    rest = jnp.concatenate([field[:half, 2 * LANES :], field[half:, 2 * LANES :]], axis=1)
    return jnp.concatenate([field[:, :LANES], field[:, LANES : 2 * LANES], rest], axis=0)


def unpack(packed):
    n = packed.shape[0] * 2 // 5
    rest = packed[2 * n :]
    tail = C - 2 * LANES
    rest = jnp.concatenate([rest[:, :tail], rest[:, tail:]], axis=0)
    return jnp.concatenate([packed[:n], packed[n : 2 * n], rest], axis=1)


def rows_at(starts, k):
    return pl.ds(starts[k] * 5 // 2, (starts[k + 1] - starts[k]) * 5 // 2)


def joined_dot(pieces, weights):
    cut = 2 * LANES
    left = jnp.concatenate([p[:, :cut] for p in pieces] + [p[:, cut:] for p in pieces], axis=1)
    right = jnp.concatenate([m[:cut] for m in weights] + [m[cut:] for m in weights], axis=0)
    return jnp.dot(left, right, preferred_element_type=F32)


def exact_dot(rows, ones):
    high = rows.astype(BF16).astype(F32)
    rest = rows - high
    middle = rest.astype(BF16).astype(F32)
    low = rest - middle
    parts = jnp.concatenate([high, middle, low, jnp.zeros_like(low)], axis=0)
    product = jnp.dot(parts.astype(BF16), ones, preferred_element_type=F32)
    return product[0:2] + product[2:4] + product[4:6]


def silu(field):
    half = 0.5 * field
    return half + half * jnp.tanh(half)


def kernel(
    x_hbm, ws_hbm, wt_hbm, gain1_hbm, shift1_hbm, gain2_hbm, shift2_hbm, bias_hbm, starts_hbm, counts_hbm, out_hbm,
    xv, xf, rows, hrow, hcol, stat, stats, planes, acc, ws, wt, out_v,
    send, got, passing,
    gain1, shift1, gain2, shift2, bias, starts, counts, x_sem, w_sem, small_sem, out_sem, near_sem, far_sem, col_ssem, col_rsem, row_ssem, row_rsem, st_ssem, st_rsem, win_ssem, win_rsem, pass_ssem, pass_rsem,
):
    w = lax.axis_index("win")
    t = lax.axis_index("tile")
    r = t // TCOLS
    q = t % TCOLS
    up, down, left, right = r > 0, r < TROWS - 1, q > 0, q < TCOLS - 1
    first, last = w == 0, w == WINDOWS - 1
    x = w % 4
    has_prev, has_next = w > 0, w < WINDOWS - 1
    far_next = (x == 3) & has_next
    far_prev = (x == 0) & has_prev
    relay_up = (x == 2) & (w + 2 < WINDOWS)
    relay_down = (x == 1) & (w - 2 >= 0)

    x_copies = [
        pltpu.make_async_copy(x_hbm.at[:, c], xv.at[c], x_sem.at[c]) for c in range(COLS)
    ]
    for copy in x_copies:
        copy.start()
    ws_copy = pltpu.make_async_copy(ws_hbm, ws, w_sem.at[0])
    wt_copy = pltpu.make_async_copy(wt_hbm, wt, w_sem.at[1])
    ws_copy.start()
    wt_copy.start()

    small = [(gain1_hbm, gain1), (shift1_hbm, shift1), (gain2_hbm, gain2), (shift2_hbm, shift2),
             (bias_hbm, bias), (starts_hbm, starts), (counts_hbm, counts)]
    small_copies = [
        pltpu.make_async_copy(src, dst, small_sem.at[i]) for i, (src, dst) in enumerate(small)
    ]
    for copy in small_copies:
        copy.start()

    barrier = pltpu.get_barrier_semaphore()
    peers = [(w, (t + i) % TILES) for i in range(1, TILES)]
    greets = [
        (has_prev, w - 1),
        (has_next, w + 1),
        (relay_up | far_next, w + 2),
        (relay_down | far_prev, w - 2),
    ]

    core, chip = t % 2, t // 2
    chips = TILES // 2
    is_near = [jnp.abs(k - chip) <= 2 for k in range(chips)]
    for k in range(chips):

        @pl.when(chip != k)
        def _(k=k):
            at = 2 * k + jnp.where(is_near[k], 1, 0)
            pl.semaphore_signal(barrier, inc=1, device_id=(w, at), device_id_type=MESH)

    @pl.when(core == 0)
    def _():
        pl.semaphore_signal(barrier, inc=1, device_id=(w, t + 1), device_id_type=MESH)

    for condition, other in greets:

        @pl.when(condition)
        def _(other=other):
            pl.semaphore_signal(barrier, inc=1, device_id=(other, t - core), device_id_type=MESH)

    near_count = 2 * sum(jnp.where(near, 1, 0) for near in is_near) - 1
    far_count = 2 * sum(jnp.where(near, 0, 1) for near in is_near) + 2 * sum(
        jnp.where(condition, 1, 0) for condition, _ in greets
    )

    per = C // GROUPS
    group_of = lax.broadcasted_iota(jnp.int32, (C, 128), 0) // per
    to_groups = (group_of == lax.broadcasted_iota(jnp.int32, (C, 128), 1)).astype(F32).astype(BF16)
    channel_group = lax.broadcasted_iota(jnp.int32, (128, C), 1) // per
    to_channels = (
        (channel_group == lax.broadcasted_iota(jnp.int32, (128, C), 0)).astype(F32).astype(BF16)
    )

    for copy in x_copies:
        copy.wait()
    total = jnp.zeros((1, C), F32)
    square = jnp.zeros((1, C), F32)
    split = jnp.transpose(xv[...].reshape(PIX, 2, C).astype(F32), (1, 0, 2))
    for y in range(2):
        plane = split[y]
        xf[y] = plane
        for k in range(len(ROW_CHUNKS)):
            part = plane[ROW_STARTS[k] : ROW_STARTS[k + 1]]
            rows[y, rows_at(ROW_STARTS, k)] = pack(part).astype(BF16)
        total = total + jnp.sum(plane, axis=0, keepdims=True)
        square = square + jnp.sum(plane * plane, axis=0, keepdims=True)

    @pl.when(core == 1)
    def _():
        pl.semaphore_wait(barrier, near_count)
        pl.semaphore_signal(near_sem, inc=1, device_id=(w, t - 1), device_id_type=MESH)

    @pl.when(core == 0)
    def _():
        pl.semaphore_wait(near_sem, 1)

    def remote(src, dst, ssem, rsem, device):
        return pltpu.make_async_remote_copy(
            src_ref=src, dst_ref=dst, send_sem=ssem, recv_sem=rsem,
            device_id=device, device_id_type=MESH,
        )

    def stat_copies(which):
        return [
            remote(stat.at[which], stats.at[which, i], st_ssem.at[which, i], st_rsem.at[which, i], peers[i])
            for i in range(TILES - 1)
        ]

    lefts, rights = xv.at[0], xv.at[COLS - 1]
    col_plan = [
        (right, rights, 1, left),
        (left, lefts, -1, right),
        (right & down, rights, TCOLS + 1, left & up),
        (left & down, lefts, TCOLS - 1, right & up),
        (right & up, rights, 1 - TCOLS, left & down),
        (left & up, lefts, -1 - TCOLS, right & down),
    ]
    col_copies = [
        remote(src, hcol.at[i], col_ssem.at[i], col_rsem.at[i], (w, (t + by + TILES) % TILES))
        for i, (_, src, by, _) in enumerate(col_plan)
    ]
    row_plan = [(down, 1, TCOLS, up), (up, 0, -TCOLS, down)]
    row_copies = [
        [
            remote(
                rows.at[y, rows_at(ROW_STARTS, k)], hrow.at[i, rows_at(ROW_STARTS, k)],
                row_ssem.at[i, k], row_rsem.at[i, k], (w, (t + by + TILES) % TILES),
            )
            for i, (_, y, by, _) in enumerate(row_plan)
        ]
        for k in range(len(ROW_CHUNKS))
    ]

    def guarded(condition, *actions):
        @pl.when(condition)
        def _():
            for action in actions:
                action()

    for i in range(2):
        guarded(row_plan[i][0], row_copies[0][i].start)

    stat[0] = exact_dot(jnp.concatenate([total, square], axis=0), to_groups)

    @pl.when(core == 0)
    def _():
        pl.semaphore_wait(barrier, far_count)
        pl.semaphore_signal(far_sem, inc=1, device_id=(w, t + 1), device_id_type=MESH)

    @pl.when(core == 1)
    def _():
        pl.semaphore_wait(far_sem, 1)

    first_stats = stat_copies(0)
    for copy in first_stats:
        copy.start()
    for i in range(6):
        guarded(col_plan[i][0], col_copies[i].start)
    for k in range(1, len(ROW_CHUNKS)):
        for i in range(2):
            guarded(row_plan[i][0], row_copies[k][i].start)

    def finish_stats(which, copies):
        for copy in copies:
            copy.wait()
        totals = stat[which]
        for i in range(TILES - 1):
            totals = totals + stats[which, i]
        mean = totals[0:1] / MEMBERS
        spread = totals[1:2] / MEMBERS - mean * mean
        inverse = lax.rsqrt(spread + EPSILON)
        spread_out = exact_dot(jnp.concatenate([mean, inverse], axis=0), to_channels)
        return spread_out[0:1], spread_out[1:2]

    mean1, inverse1 = finish_stats(0, first_stats)
    for copy in small_copies:
        copy.wait()
    scale1 = inverse1 * gain1[...].reshape(1, C)
    offset1 = shift1[...].reshape(1, C)

    def act(field):
        return silu((field - mean1) * scale1 + offset1).astype(BF16)

    for y in range(2):
        planes[1 + y, FRAMES : FRAMES + PIX] = act(xf[y])

    empty = jnp.zeros((FRAMES, C), BF16)
    places = [0, FRAMES * (COLS + 1)]
    for i in range(2):
        guarded(col_plan[i][3], col_copies[i].wait_recv)
        at = places[i]

        @pl.when(col_plan[i][3])
        def _(i=i, at=at):
            both = jnp.transpose(hcol[i].astype(F32), (1, 0, 2))
            for y in range(2):
                planes[1 + y, at : at + FRAMES] = act(both[y])

        @pl.when(jnp.logical_not(col_plan[i][3]))
        def _(at=at):
            for y in range(2):
                planes[1 + y, at : at + FRAMES] = empty

    for i in range(2, 6):
        guarded(col_plan[i][3], col_copies[i].wait_recv)
        at = places[i % 2]
        plane, y = (0, 1) if i < 4 else (3, 0)

        @pl.when(col_plan[i][3])
        def _(i=i, at=at, plane=plane, y=y):
            both = jnp.transpose(hcol[i].astype(F32), (1, 0, 2))
            planes[plane, at : at + FRAMES] = act(both[y])

        @pl.when(jnp.logical_not(col_plan[i][3]))
        def _(at=at, plane=plane):
            planes[plane, at : at + FRAMES] = empty

    ws_copy.wait()

    def taps(y, rows):
        pairs = [(a, b) for a in rows for b in range(3)]
        return joined_dot(
            [planes[y + a, FRAMES * b : FRAMES * b + PIX] for a, b in pairs], [ws[a, b] for a, b in pairs]
        )

    acc[0] = taps(0, (1, 2))
    acc[1] = taps(1, (0, 1))

    for i in range(2):
        plane = 0 if i == 0 else 3

        @pl.when(row_plan[i][3])
        def _(i=i, plane=plane):
            for k in range(len(ROW_CHUNKS)):
                row_copies[k][i].wait_recv()
                arrived = unpack(hrow[i, rows_at(ROW_STARTS, k)].astype(F32))
                planes[plane, FRAMES + ROW_STARTS[k] : FRAMES + ROW_STARTS[k + 1]] = act(arrived)

        @pl.when(jnp.logical_not(row_plan[i][3]))
        def _(plane=plane):
            planes[plane, FRAMES : FRAMES + PIX] = jnp.zeros((PIX, C), BF16)

    total = jnp.zeros((1, C), F32)
    square = jnp.zeros((1, C), F32)
    for y in range(2):
        spatial = (acc[y] + taps(y, (2 * y,))).astype(BF16).astype(F32)
        acc[y] = spatial
        total = total + jnp.sum(spatial, axis=0, keepdims=True)
        square = square + jnp.sum(spatial * spatial, axis=0, keepdims=True)
    stat[1] = exact_dot(jnp.concatenate([total, square], axis=0), to_groups)
    second_stats = stat_copies(1)
    for copy in second_stats:
        copy.start()

    lane_window = lax.broadcasted_iota(jnp.int32, (FRAMES, WINDOWS), 1)
    held = counts[...]

    def counts_of(index):
        return jnp.sum(jnp.where(lane_window == index, held, 0), axis=1, keepdims=True)

    start_lane = lax.broadcasted_iota(jnp.int32, (1, WINDOWS), 1)

    def start_of(index):
        return jnp.sum(jnp.where(start_lane == index, starts[...].reshape(1, WINDOWS), 0), axis=1, keepdims=True)

    side = SIDE
    lane = lax.broadcasted_iota(jnp.int32, (side * FRAMES, side * FRAMES), 1)
    row = lax.broadcasted_iota(jnp.int32, (side * FRAMES, side * FRAMES), 0)
    frame = row % FRAMES
    from_prev = lane < side * SHARED
    slot = lane % SHARED
    same = row // FRAMES == (lane // SHARED) % side
    gap_prev = start_of(w) - start_of(w - 1)
    gap_next = start_of(w + 1) - start_of(w)
    wanted = jnp.where(from_prev, frame + gap_prev - (FRAMES - SHARED), frame - gap_next)
    exists = jnp.where(from_prev, jnp.where(first, 0, 1), jnp.where(last, 0, 1)) > 0
    lane16 = lax.broadcasted_iota(jnp.int32, (FRAMES, side * FRAMES), 1)
    frame16 = lax.broadcasted_iota(jnp.int32, (FRAMES, side * FRAMES), 0)
    prev_lanes = lane16 < side * SHARED
    at_frame = frame16 == lane16 % SHARED + jnp.where(prev_lanes, FRAMES - SHARED, 0)
    lane_counts = jnp.sum(
        jnp.where(at_frame, jnp.where(prev_lanes, counts_of(w - 1), counts_of(w + 1)), 0),
        axis=0,
        keepdims=True,
    )
    blend = jnp.where(same & exists & (slot == wanted), lane_counts, 0).astype(F32)
    own = jnp.concatenate([counts_of(w).astype(F32)] * side, axis=0)
    denominator = own + jnp.sum(blend, axis=1, keepdims=True)
    blend_matrix = blend.astype(BF16)

    mean2, inverse2 = finish_stats(1, second_stats)
    scale2 = inverse2 * gain2[...].reshape(1, C)
    offset2 = shift2[...].reshape(1, C)

    wt_copy.wait()
    frame_at = lax.broadcasted_iota(jnp.int32, (PIX, 1), 0) % FRAMES
    def window(index):
        return (lax.clamp(0, index, WINDOWS - 1), t)

    direct, aside, onward = [], [], []
    for k in range(len(CHUNKS)):
        at = rows_at(STARTS, k)
        direct.append([
            remote(send.at[0, at], got.at[1, at], win_ssem.at[0, k], win_rsem.at[0, k], window(w - 1)),
            remote(send.at[1, at], got.at[0, at], win_ssem.at[1, k], win_rsem.at[1, k], window(w + 1)),
        ])
        if k < PASSED:
            aside.append([
                remote(send.at[0, at], passing.at[at], win_ssem.at[0, k], pass_rsem.at[k], window(w + 1)),
                remote(send.at[1, at], passing.at[at], win_ssem.at[1, k], pass_rsem.at[k], window(w - 1)),
            ])
            onward.append([
                remote(passing.at[at], got.at[1, at], pass_ssem.at[k], win_rsem.at[0, k], window(w - 2)),
                remote(passing.at[at], got.at[0, at], pass_ssem.at[k], win_rsem.at[1, k], window(w + 2)),
            ])

    def send_chunk(k):
        if k < PASSED:
            guarded(has_prev & jnp.logical_not(far_prev), direct[k][0].start)
            guarded(has_next & jnp.logical_not(far_next), direct[k][1].start)
            guarded(far_prev, aside[k][0].start)
            guarded(far_next, aside[k][1].start)
        else:
            guarded(has_prev, direct[k][0].start)
            guarded(has_next, direct[k][1].start)

    @pl.when(first)
    def _():
        got[0] = jnp.zeros_like(got[0])

    @pl.when(last)
    def _():
        got[1] = jnp.zeros_like(got[1])

    frame_rows = COLS * SHARED
    left_over, done = None, 0
    for y in range(2):
        mixed = silu((acc[y] - mean2) * scale2 + offset2)
        before = jnp.where(frame_at > 0, pltpu.roll(mixed, 1, 0), 0.0)
        after = jnp.where(frame_at < FRAMES - 1, pltpu.roll(mixed, PIX - 1, 0), 0.0)
        running = xf[y] + bias[...].reshape(1, C) + joined_dot(
            [before.astype(BF16), mixed.astype(BF16), after.astype(BF16)], [wt[k] for k in range(3)]
        )
        block = running.astype(BF16).astype(F32)
        acc[y] = block
        halves = block.reshape(COLS, 2, SHARED, C)
        dense = [halves[:, part].reshape(frame_rows, C) for part in range(2)]
        if left_over is not None:
            dense = [jnp.concatenate([left_over[part], dense[part]], axis=0) for part in range(2)]
        base = 0 if y == 0 else STARTS[done]
        for k in range(done, len(CHUNKS)):
            if STARTS[k + 1] > frame_rows * (y + 1):
                break
            for part in range(2):
                chunk = dense[part][STARTS[k] - base : STARTS[k + 1] - base]
                send[part, rows_at(STARTS, k)] = pack(chunk).astype(BF16)
            send_chunk(k)
            done = k + 1
        if STARTS[done] < frame_rows * (y + 1):
            left_over = [dense[part][STARTS[done] - base :] for part in range(2)]
        else:
            left_over = None
    for k in range(PASSED):
        guarded(relay_down, aside[k][0].wait_recv, onward[k][0].start)
        guarded(relay_up, aside[k][1].wait_recv, onward[k][1].start)

    for (sends, _, _, _), copy in zip(col_plan, col_copies):
        guarded(sends, copy.wait_send)
    for k in range(len(ROW_CHUNKS)):
        for i in range(2):
            guarded(row_plan[i][0], row_copies[k][i].wait_send)
    for k in range(len(CHUNKS)):
        guarded(has_prev, direct[k][1].wait_recv, direct[k][0].wait_send)
        guarded(has_next, direct[k][0].wait_recv, direct[k][1].wait_send)
    for k in range(PASSED):
        guarded(relay_down, onward[k][0].wait_send)
        guarded(relay_up, onward[k][1].wait_send)

    share = 1.0 / denominator
    depth = side * SHARED

    def whole(part):
        return jnp.concatenate([unpack(got[part, rows_at(STARTS, k)]) for k in range(len(CHUNKS))], axis=0)

    prev_all, next_all = whole(0), whole(1)
    own_all = acc[...].reshape(2 * PIX, C)
    height = side * FRAMES
    out_copies = [
        pltpu.make_async_copy(
            out_v.at[pl.ds(k * height, height)], out_hbm.at[pl.ds(k * height, height)], out_sem.at[k]
        )
        for k in range(5)
    ]
    for k in range(5):
        others = jnp.concatenate(
            [prev_all[k * depth : (k + 1) * depth], next_all[k * depth : (k + 1) * depth]], axis=0
        )
        numerator = jnp.dot(blend_matrix, others, preferred_element_type=F32)
        numerator = numerator + own * own_all[k * height : (k + 1) * height]
        result = numerator * share
        out_v[k * height : (k + 1) * height] = result.astype(BF16)
        out_copies[k].start()
    for copy in out_copies:
        copy.wait()


def on_device(
    latents, spatial_weight, temporal_weight, gain_first, shift_first, gain_second, shift_second,
    temporal_bias, starts, blend_counts,
):
    x = jnp.transpose(latents.reshape(FRAMES, 2, COLS, C), (0, 2, 1, 3))
    hbm = pl.BlockSpec(memory_space=pltpu.HBM)
    dma = pltpu.SemaphoreType.DMA
    out = pl.pallas_call(
        kernel,
        out_shape=jax.ShapeDtypeStruct((2 * PIX, C), BF16),
        in_specs=[hbm] * 10,
        out_specs=hbm,
        scratch_shapes=[
            pltpu.VMEM((COLS, FRAMES, 2, C), BF16),
            pltpu.VMEM((2, PIX, C), F32),
            pltpu.VMEM((2, PACKED, LANES), BF16),
            pltpu.VMEM((2, PACKED, LANES), BF16),
            pltpu.VMEM((6, FRAMES, 2, C), BF16),
            pltpu.VMEM((2, 2, 128), F32),
            pltpu.VMEM((2, TILES - 1, 2, 128), F32),
            pltpu.VMEM((4, WIDE, C), BF16),
            pltpu.VMEM((2, PIX, C), F32),
            pltpu.VMEM((3, 3, C, C), BF16),
            pltpu.VMEM((3, C, C), BF16),
            pltpu.VMEM((2 * PIX, C), BF16),
            pltpu.VMEM((2, PACKED, LANES), BF16),
            pltpu.VMEM((2, PACKED, LANES), BF16),
            pltpu.VMEM((STARTS[PASSED] * 5 // 2, LANES), BF16),
            pltpu.VMEM((C,), F32),
            pltpu.VMEM((C,), F32),
            pltpu.VMEM((C,), F32),
            pltpu.VMEM((C,), F32),
            pltpu.VMEM((C,), F32),
            pltpu.VMEM((WINDOWS,), jnp.int32),
            pltpu.VMEM((FRAMES, WINDOWS), jnp.int32),
            dma((COLS,)),
            dma((2,)),
            dma((7,)),
            dma((COLS,)),
            pltpu.SemaphoreType.REGULAR,
            pltpu.SemaphoreType.REGULAR,
            dma((6,)),
            dma((6,)),
            dma((2, len(ROW_CHUNKS))),
            dma((2, len(ROW_CHUNKS))),
            dma((2, TILES - 1)),
            dma((2, TILES - 1)),
            dma((2, len(CHUNKS))),
            dma((2, len(CHUNKS))),
            dma((PASSED,)),
            dma((PASSED,)),
        ],
        compiler_params=pltpu.CompilerParams(
            collective_id=0, has_side_effects=True, vmem_limit_bytes=60 << 20
        ),
        cost_estimate=pl.CostEstimate(flops=1_600_000_000, bytes_accessed=4_000_000, transcendentals=400_000),
        name="resblock",
    )(
        x, spatial_weight, temporal_weight, gain_first, shift_first, gain_second, shift_second,
        temporal_bias, starts, blend_counts.T,
    )
    return jnp.transpose(out.reshape(2, COLS, FRAMES, C), (2, 0, 1, 3)).reshape(1, FRAMES, 1, 2, COLS, C)


def solution(mesh):
    return jax.shard_map(
        on_device,
        mesh=mesh,
        in_specs=(P("win", None, "tile", None, None, None),) + (P(),) * 9,
        out_specs=P("win", None, "tile", None, None, None),
        check_vma=False,
    )
```

```python
import jax
import jax.numpy as jnp
from jax import lax
from jax.experimental import pallas as pl
from jax.experimental.pallas import tpu as pltpu
from jax.sharding import PartitionSpec as P

MESH = pl.DeviceIdType.MESH
F32 = jnp.float32
BF16 = jnp.bfloat16

GROUPS = 32
EPSILON = 1e-05
FRAMES = 16
SHARED = 8
TCOLS = 4
TROWS = 4
TILES = TCOLS * TROWS
WINDOWS = 32
COLS = 20
C = 320
LANES = 128
PIX = COLS * FRAMES
WIDE = (COLS + 2) * FRAMES
PACKED = PIX * 5 // 2
SIDE = 8
CHUNKS = (64, 64, 32, 160)
PASSED = 2
STARTS = tuple(sum(CHUNKS[:i]) for i in range(len(CHUNKS) + 1))
ROW_CHUNKS = (64, 256)
ROW_STARTS = (0, 64, 320)
MEMBERS = float(FRAMES * TILES * 2 * COLS * (C // GROUPS))


def pack(field):
    half = field.shape[0] // 2
    rest = jnp.concatenate([field[:half, 2 * LANES :], field[half:, 2 * LANES :]], axis=1)
    return jnp.concatenate([field[:, :LANES], field[:, LANES : 2 * LANES], rest], axis=0)


def unpack(packed):
    n = packed.shape[0] * 2 // 5
    rest = packed[2 * n :]
    tail = C - 2 * LANES
    rest = jnp.concatenate([rest[:, :tail], rest[:, tail:]], axis=0)
    return jnp.concatenate([packed[:n], packed[n : 2 * n], rest], axis=1)


def rows_at(starts, k):
    return pl.ds(starts[k] * 5 // 2, (starts[k + 1] - starts[k]) * 5 // 2)


def joined_dot(pieces, weights):
    cut = 2 * LANES
    left = jnp.concatenate([p[:, :cut] for p in pieces] + [p[:, cut:] for p in pieces], axis=1)
    right = jnp.concatenate([m[:cut] for m in weights] + [m[cut:] for m in weights], axis=0)
    return jnp.dot(left, right, preferred_element_type=F32)


def exact_dot(rows, ones):
    high = rows.astype(BF16).astype(F32)
    rest = rows - high
    middle = rest.astype(BF16).astype(F32)
    low = rest - middle
    parts = jnp.concatenate([high, middle, low, jnp.zeros_like(low)], axis=0)
    product = jnp.dot(parts.astype(BF16), ones, preferred_element_type=F32)
    return product[0:2] + product[2:4] + product[4:6]


def silu(field):
    half = 0.5 * field
    return half + half * jnp.tanh(half)


def kernel(
    x_hbm, ws_hbm, wt_hbm, gain1_hbm, shift1_hbm, gain2_hbm, shift2_hbm, bias_hbm, starts_hbm, counts_hbm, out_hbm,
    xv, xf, rows, hrow, hcol, stat, stats, planes, acc, ws, wt, out_v,
    send, got, passing,
    gain1, shift1, gain2, shift2, bias, starts, counts, x_sem, w_sem, small_sem, out_sem, near_sem, far_sem, col_ssem, col_rsem, row_ssem, row_rsem, st_ssem, st_rsem, win_ssem, win_rsem, pass_ssem, pass_rsem,
):
    w = lax.axis_index("win")
    t = lax.axis_index("tile")
    r = t // TCOLS
    q = t % TCOLS
    up, down, left, right = r > 0, r < TROWS - 1, q > 0, q < TCOLS - 1
    first, last = w == 0, w == WINDOWS - 1
    x = w % 4
    has_prev, has_next = w > 0, w < WINDOWS - 1
    far_next = (x == 3) & has_next
    far_prev = (x == 0) & has_prev
    relay_up = (x == 2) & (w + 2 < WINDOWS)
    relay_down = (x == 1) & (w - 2 >= 0)

    x_copies = [
        pltpu.make_async_copy(x_hbm.at[:, c], xv.at[c], x_sem.at[c]) for c in range(COLS)
    ]
    for copy in x_copies:
        copy.start()
    ws_copy = pltpu.make_async_copy(ws_hbm, ws, w_sem.at[0])
    wt_copy = pltpu.make_async_copy(wt_hbm, wt, w_sem.at[1])
    ws_copy.start()
    wt_copy.start()

    small = [(gain1_hbm, gain1), (shift1_hbm, shift1), (gain2_hbm, gain2), (shift2_hbm, shift2),
             (bias_hbm, bias), (starts_hbm, starts), (counts_hbm, counts)]
    small_copies = [
        pltpu.make_async_copy(src, dst, small_sem.at[i]) for i, (src, dst) in enumerate(small)
    ]
    for copy in small_copies:
        copy.start()

    barrier = pltpu.get_barrier_semaphore()
    peers = [(w, (t + i) % TILES) for i in range(1, TILES)]
    greets = [
        (has_prev, w - 1),
        (has_next, w + 1),
        (relay_up | far_next, w + 2),
        (relay_down | far_prev, w - 2),
    ]

    core, chip = t % 2, t // 2
    chips = TILES // 2
    is_near = [jnp.abs(k - chip) <= 2 for k in range(chips)]
    for k in range(chips):

        @pl.when(chip != k)
        def _(k=k):
            at = 2 * k + jnp.where(is_near[k], 1, 0)
            pl.semaphore_signal(barrier, inc=1, device_id=(w, at), device_id_type=MESH)

    @pl.when(core == 0)
    def _():
        pl.semaphore_signal(barrier, inc=1, device_id=(w, t + 1), device_id_type=MESH)

    for condition, other in greets:

        @pl.when(condition)
        def _(other=other):
            pl.semaphore_signal(barrier, inc=1, device_id=(other, t - core), device_id_type=MESH)

    near_count = 2 * sum(jnp.where(near, 1, 0) for near in is_near) - 1
    far_count = 2 * sum(jnp.where(near, 0, 1) for near in is_near) + 2 * sum(
        jnp.where(condition, 1, 0) for condition, _ in greets
    )

    per = C // GROUPS
    group_of = lax.broadcasted_iota(jnp.int32, (C, 128), 0) // per
    to_groups = (group_of == lax.broadcasted_iota(jnp.int32, (C, 128), 1)).astype(F32).astype(BF16)
    channel_group = lax.broadcasted_iota(jnp.int32, (128, C), 1) // per
    to_channels = (
        (channel_group == lax.broadcasted_iota(jnp.int32, (128, C), 0)).astype(F32).astype(BF16)
    )

    for copy in x_copies:
        copy.wait()
    total = jnp.zeros((1, C), F32)
    square = jnp.zeros((1, C), F32)
    split = jnp.transpose(xv[...].reshape(PIX, 2, C).astype(F32), (1, 0, 2))
    for y in range(2):
        plane = split[y]
        xf[y] = plane
        for k in range(len(ROW_CHUNKS)):
            part = plane[ROW_STARTS[k] : ROW_STARTS[k + 1]]
            rows[y, rows_at(ROW_STARTS, k)] = pack(part).astype(BF16)
        total = total + jnp.sum(plane, axis=0, keepdims=True)
        square = square + jnp.sum(plane * plane, axis=0, keepdims=True)

    @pl.when(core == 1)
    def _():
        pl.semaphore_wait(barrier, near_count)
        pl.semaphore_signal(near_sem, inc=1, device_id=(w, t - 1), device_id_type=MESH)

    @pl.when(core == 0)
    def _():
        pl.semaphore_wait(near_sem, 1)

    def remote(src, dst, ssem, rsem, device):
        return pltpu.make_async_remote_copy(
            src_ref=src, dst_ref=dst, send_sem=ssem, recv_sem=rsem,
            device_id=device, device_id_type=MESH,
        )

    def stat_copies(which):
        return [
            remote(stat.at[which], stats.at[which, i], st_ssem.at[which, i], st_rsem.at[which, i], peers[i])
            for i in range(TILES - 1)
        ]

    lefts, rights = xv.at[0], xv.at[COLS - 1]
    col_plan = [
        (right, rights, 1, left),
        (left, lefts, -1, right),
        (right & down, rights, TCOLS + 1, left & up),
        (left & down, lefts, TCOLS - 1, right & up),
        (right & up, rights, 1 - TCOLS, left & down),
        (left & up, lefts, -1 - TCOLS, right & down),
    ]
    col_copies = [
        remote(src, hcol.at[i], col_ssem.at[i], col_rsem.at[i], (w, (t + by + TILES) % TILES))
        for i, (_, src, by, _) in enumerate(col_plan)
    ]
    row_plan = [(down, 1, TCOLS, up), (up, 0, -TCOLS, down)]
    row_copies = [
        [
            remote(
                rows.at[y, rows_at(ROW_STARTS, k)], hrow.at[i, rows_at(ROW_STARTS, k)],
                row_ssem.at[i, k], row_rsem.at[i, k], (w, (t + by + TILES) % TILES),
            )
            for i, (_, y, by, _) in enumerate(row_plan)
        ]
        for k in range(len(ROW_CHUNKS))
    ]

    def guarded(condition, *actions):
        @pl.when(condition)
        def _():
            for action in actions:
                action()

    for i in range(2):
        guarded(row_plan[i][0], row_copies[0][i].start)

    stat[0] = exact_dot(jnp.concatenate([total, square], axis=0), to_groups)

    @pl.when(core == 0)
    def _():
        pl.semaphore_wait(barrier, far_count)
        pl.semaphore_signal(far_sem, inc=1, device_id=(w, t + 1), device_id_type=MESH)

    @pl.when(core == 1)
    def _():
        pl.semaphore_wait(far_sem, 1)

    first_stats = stat_copies(0)
    for copy in first_stats:
        copy.start()
    for i in range(6):
        guarded(col_plan[i][0], col_copies[i].start)
    for k in range(1, len(ROW_CHUNKS)):
        for i in range(2):
            guarded(row_plan[i][0], row_copies[k][i].start)

    def finish_stats(which, copies):
        for copy in copies:
            copy.wait()
        totals = stat[which]
        for i in range(TILES - 1):
            totals = totals + stats[which, i]
        mean = totals[0:1] / MEMBERS
        spread = totals[1:2] / MEMBERS - mean * mean
        inverse = lax.rsqrt(spread + EPSILON)
        spread_out = exact_dot(jnp.concatenate([mean, inverse], axis=0), to_channels)
        return spread_out[0:1], spread_out[1:2]

    mean1, inverse1 = finish_stats(0, first_stats)
    for copy in small_copies:
        copy.wait()
    scale1 = inverse1 * gain1[...].reshape(1, C)
    offset1 = shift1[...].reshape(1, C)

    def act(field):
        return silu((field - mean1) * scale1 + offset1).astype(BF16)

    for y in range(2):
        planes[1 + y, FRAMES : FRAMES + PIX] = act(xf[y])

    empty = jnp.zeros((FRAMES, C), BF16)
    places = [0, FRAMES * (COLS + 1)]
    for i in range(2):
        guarded(col_plan[i][3], col_copies[i].wait_recv)
        at = places[i]

        @pl.when(col_plan[i][3])
        def _(i=i, at=at):
            both = jnp.transpose(hcol[i].astype(F32), (1, 0, 2))
            for y in range(2):
                planes[1 + y, at : at + FRAMES] = act(both[y])

        @pl.when(jnp.logical_not(col_plan[i][3]))
        def _(at=at):
            for y in range(2):
                planes[1 + y, at : at + FRAMES] = empty

    for i in range(2, 6):
        guarded(col_plan[i][3], col_copies[i].wait_recv)
        at = places[i % 2]
        plane, y = (0, 1) if i < 4 else (3, 0)

        @pl.when(col_plan[i][3])
        def _(i=i, at=at, plane=plane, y=y):
            both = jnp.transpose(hcol[i].astype(F32), (1, 0, 2))
            planes[plane, at : at + FRAMES] = act(both[y])

        @pl.when(jnp.logical_not(col_plan[i][3]))
        def _(at=at, plane=plane):
            planes[plane, at : at + FRAMES] = empty

    ws_copy.wait()

    def taps(y, rows):
        pairs = [(a, b) for a in rows for b in range(3)]
        return joined_dot(
            [planes[y + a, FRAMES * b : FRAMES * b + PIX] for a, b in pairs], [ws[a, b] for a, b in pairs]
        )

    acc[0] = taps(0, (1, 2))
    acc[1] = taps(1, (0, 1))

    for i in range(2):
        plane = 0 if i == 0 else 3

        @pl.when(row_plan[i][3])
        def _(i=i, plane=plane):
            for k in range(len(ROW_CHUNKS)):
                row_copies[k][i].wait_recv()
                arrived = unpack(hrow[i, rows_at(ROW_STARTS, k)].astype(F32))
                planes[plane, FRAMES + ROW_STARTS[k] : FRAMES + ROW_STARTS[k + 1]] = act(arrived)

        @pl.when(jnp.logical_not(row_plan[i][3]))
        def _(plane=plane):
            planes[plane, FRAMES : FRAMES + PIX] = jnp.zeros((PIX, C), BF16)

    total = jnp.zeros((1, C), F32)
    square = jnp.zeros((1, C), F32)
    for y in range(2):
        spatial = (acc[y] + taps(y, (2 * y,))).astype(BF16).astype(F32)
        acc[y] = spatial
        total = total + jnp.sum(spatial, axis=0, keepdims=True)
        square = square + jnp.sum(spatial * spatial, axis=0, keepdims=True)
    stat[1] = exact_dot(jnp.concatenate([total, square], axis=0), to_groups)
    second_stats = stat_copies(1)
    for copy in second_stats:
        copy.start()

    lane_window = lax.broadcasted_iota(jnp.int32, (FRAMES, WINDOWS), 1)
    held = counts[...]

    def counts_of(index):
        return jnp.sum(jnp.where(lane_window == index, held, 0), axis=1, keepdims=True)

    start_lane = lax.broadcasted_iota(jnp.int32, (1, WINDOWS), 1)

    def start_of(index):
        return jnp.sum(jnp.where(start_lane == index, starts[...].reshape(1, WINDOWS), 0), axis=1, keepdims=True)

    side = SIDE
    lane = lax.broadcasted_iota(jnp.int32, (side * FRAMES, side * FRAMES), 1)
    row = lax.broadcasted_iota(jnp.int32, (side * FRAMES, side * FRAMES), 0)
    frame = row % FRAMES
    from_prev = lane < side * SHARED
    slot = lane % SHARED
    same = row // FRAMES == (lane // SHARED) % side
    gap_prev = start_of(w) - start_of(w - 1)
    gap_next = start_of(w + 1) - start_of(w)
    wanted = jnp.where(from_prev, frame + gap_prev - (FRAMES - SHARED), frame - gap_next)
    exists = jnp.where(from_prev, jnp.where(first, 0, 1), jnp.where(last, 0, 1)) > 0
    lane16 = lax.broadcasted_iota(jnp.int32, (FRAMES, side * FRAMES), 1)
    frame16 = lax.broadcasted_iota(jnp.int32, (FRAMES, side * FRAMES), 0)
    prev_lanes = lane16 < side * SHARED
    at_frame = frame16 == lane16 % SHARED + jnp.where(prev_lanes, FRAMES - SHARED, 0)
    lane_counts = jnp.sum(
        jnp.where(at_frame, jnp.where(prev_lanes, counts_of(w - 1), counts_of(w + 1)), 0),
        axis=0,
        keepdims=True,
    )
    blend = jnp.where(same & exists & (slot == wanted), lane_counts, 0).astype(F32)
    own = jnp.concatenate([counts_of(w).astype(F32)] * side, axis=0)
    denominator = own + jnp.sum(blend, axis=1, keepdims=True)
    blend_matrix = blend.astype(BF16)

    mean2, inverse2 = finish_stats(1, second_stats)
    scale2 = inverse2 * gain2[...].reshape(1, C)
    offset2 = shift2[...].reshape(1, C)

    wt_copy.wait()
    frame_at = lax.broadcasted_iota(jnp.int32, (PIX, 1), 0) % FRAMES
    def window(index):
        return (lax.clamp(0, index, WINDOWS - 1), t)

    direct, aside, onward = [], [], []
    for k in range(len(CHUNKS)):
        at = rows_at(STARTS, k)
        direct.append([
            remote(send.at[0, at], got.at[1, at], win_ssem.at[0, k], win_rsem.at[0, k], window(w - 1)),
            remote(send.at[1, at], got.at[0, at], win_ssem.at[1, k], win_rsem.at[1, k], window(w + 1)),
        ])
        if k < PASSED:
            aside.append([
                remote(send.at[0, at], passing.at[at], win_ssem.at[0, k], pass_rsem.at[k], window(w + 1)),
                remote(send.at[1, at], passing.at[at], win_ssem.at[1, k], pass_rsem.at[k], window(w - 1)),
            ])
            onward.append([
                remote(passing.at[at], got.at[1, at], pass_ssem.at[k], win_rsem.at[0, k], window(w - 2)),
                remote(passing.at[at], got.at[0, at], pass_ssem.at[k], win_rsem.at[1, k], window(w + 2)),
            ])

    far = far_prev | far_next

    def send_chunk(k):
        if k < PASSED:
            guarded(far_prev, aside[k][0].start)
            guarded(far_next, aside[k][1].start)
            guarded(has_prev & jnp.logical_not(far), direct[k][0].start)
            guarded(has_next & jnp.logical_not(far), direct[k][1].start)
        else:
            guarded(has_prev & jnp.logical_not(far_next), direct[k][0].start)
            guarded(has_next & jnp.logical_not(far_prev), direct[k][1].start)

    def send_beside(k):
        guarded(far_next, direct[k][0].start)
        guarded(far_prev, direct[k][1].start)

    @pl.when(first)
    def _():
        got[0] = jnp.zeros_like(got[0])

    @pl.when(last)
    def _():
        got[1] = jnp.zeros_like(got[1])

    frame_rows = COLS * SHARED
    left_over, done = None, 0
    for y in range(2):
        mixed = silu((acc[y] - mean2) * scale2 + offset2)
        before = jnp.where(frame_at > 0, pltpu.roll(mixed, 1, 0), 0.0)
        after = jnp.where(frame_at < FRAMES - 1, pltpu.roll(mixed, PIX - 1, 0), 0.0)
        running = xf[y] + bias[...].reshape(1, C) + joined_dot(
            [before.astype(BF16), mixed.astype(BF16), after.astype(BF16)], [wt[k] for k in range(3)]
        )
        block = running.astype(BF16).astype(F32)
        acc[y] = block
        halves = block.reshape(COLS, 2, SHARED, C)
        dense = [halves[:, part].reshape(frame_rows, C) for part in range(2)]
        if left_over is not None:
            dense = [jnp.concatenate([left_over[part], dense[part]], axis=0) for part in range(2)]
        base = 0 if y == 0 else STARTS[done]
        for k in range(done, len(CHUNKS)):
            if STARTS[k + 1] > frame_rows * (y + 1):
                break
            for part in range(2):
                chunk = dense[part][STARTS[k] - base : STARTS[k + 1] - base]
                send[part, rows_at(STARTS, k)] = pack(chunk).astype(BF16)
            send_chunk(k)
            done = k + 1
        if STARTS[done] < frame_rows * (y + 1):
            left_over = [dense[part][STARTS[done] - base :] for part in range(2)]
        else:
            left_over = None
    for k in range(len(CHUNKS)):
        send_beside(k)
    for k in range(PASSED):
        guarded(relay_down, aside[k][0].wait_recv, onward[k][0].start)
        guarded(relay_up, aside[k][1].wait_recv, onward[k][1].start)

    for (sends, _, _, _), copy in zip(col_plan, col_copies):
        guarded(sends, copy.wait_send)
    for k in range(len(ROW_CHUNKS)):
        for i in range(2):
            guarded(row_plan[i][0], row_copies[k][i].wait_send)
    share = 1.0 / denominator
    depth = side * SHARED

    own_all = acc[...].reshape(2 * PIX, C)
    height = side * FRAMES
    arrived, waited = [[], []], 0
    out_copies = [
        pltpu.make_async_copy(
            out_v.at[pl.ds(k * height, height)], out_hbm.at[pl.ds(k * height, height)], out_sem.at[k]
        )
        for k in range(5)
    ]
    for k in range(5):
        while STARTS[waited] < (k + 1) * depth:
            guarded(has_prev, direct[waited][1].wait_recv)
            guarded(has_next, direct[waited][0].wait_recv)
            for part in range(2):
                arrived[part].append(unpack(got[part, rows_at(STARTS, waited)]))
            waited += 1
        others = jnp.concatenate(
            [jnp.concatenate(arrived[part], axis=0)[k * depth : (k + 1) * depth] for part in range(2)], axis=0
        )
        numerator = jnp.dot(blend_matrix, others, preferred_element_type=F32)
        numerator = numerator + own * own_all[k * height : (k + 1) * height]
        result = numerator * share
        out_v[k * height : (k + 1) * height] = result.astype(BF16)
        out_copies[k].start()
    for copy in out_copies:
        copy.wait()
    for k in range(len(CHUNKS)):
        guarded(has_prev, direct[k][0].wait_send)
        guarded(has_next, direct[k][1].wait_send)
    for k in range(PASSED):
        guarded(relay_down, onward[k][0].wait_send)
        guarded(relay_up, onward[k][1].wait_send)


def on_device(
    latents, spatial_weight, temporal_weight, gain_first, shift_first, gain_second, shift_second,
    temporal_bias, starts, blend_counts,
):
    x = jnp.transpose(latents.reshape(FRAMES, 2, COLS, C), (0, 2, 1, 3))
    hbm = pl.BlockSpec(memory_space=pltpu.HBM)
    dma = pltpu.SemaphoreType.DMA
    out = pl.pallas_call(
        kernel,
        out_shape=jax.ShapeDtypeStruct((2 * PIX, C), BF16),
        in_specs=[hbm] * 10,
        out_specs=hbm,
        scratch_shapes=[
            pltpu.VMEM((COLS, FRAMES, 2, C), BF16),
            pltpu.VMEM((2, PIX, C), F32),
            pltpu.VMEM((2, PACKED, LANES), BF16),
            pltpu.VMEM((2, PACKED, LANES), BF16),
            pltpu.VMEM((6, FRAMES, 2, C), BF16),
            pltpu.VMEM((2, 2, 128), F32),
            pltpu.VMEM((2, TILES - 1, 2, 128), F32),
            pltpu.VMEM((4, WIDE, C), BF16),
            pltpu.VMEM((2, PIX, C), F32),
            pltpu.VMEM((3, 3, C, C), BF16),
            pltpu.VMEM((3, C, C), BF16),
            pltpu.VMEM((2 * PIX, C), BF16),
            pltpu.VMEM((2, PACKED, LANES), BF16),
            pltpu.VMEM((2, PACKED, LANES), BF16),
            pltpu.VMEM((STARTS[PASSED] * 5 // 2, LANES), BF16),
            pltpu.VMEM((C,), F32),
            pltpu.VMEM((C,), F32),
            pltpu.VMEM((C,), F32),
            pltpu.VMEM((C,), F32),
            pltpu.VMEM((C,), F32),
            pltpu.VMEM((WINDOWS,), jnp.int32),
            pltpu.VMEM((FRAMES, WINDOWS), jnp.int32),
            dma((COLS,)),
            dma((2,)),
            dma((7,)),
            dma((COLS,)),
            pltpu.SemaphoreType.REGULAR,
            pltpu.SemaphoreType.REGULAR,
            dma((6,)),
            dma((6,)),
            dma((2, len(ROW_CHUNKS))),
            dma((2, len(ROW_CHUNKS))),
            dma((2, TILES - 1)),
            dma((2, TILES - 1)),
            dma((2, len(CHUNKS))),
            dma((2, len(CHUNKS))),
            dma((PASSED,)),
            dma((PASSED,)),
        ],
        compiler_params=pltpu.CompilerParams(
            collective_id=0, has_side_effects=True, vmem_limit_bytes=60 << 20
        ),
        cost_estimate=pl.CostEstimate(flops=1_600_000_000, bytes_accessed=4_000_000, transcendentals=400_000),
        name="resblock",
    )(
        x, spatial_weight, temporal_weight, gain_first, shift_first, gain_second, shift_second,
        temporal_bias, starts, blend_counts.T,
    )
    return jnp.transpose(out.reshape(2, COLS, FRAMES, C), (2, 0, 1, 3)).reshape(1, FRAMES, 1, 2, COLS, C)


def solution(mesh):
    return jax.shard_map(
        on_device,
        mesh=mesh,
        in_specs=(P("win", None, "tile", None, None, None),) + (P(),) * 9,
        out_specs=P("win", None, "tile", None, None, None),
        check_vma=False,
    )
```
